512 devices in a mesh: seq: 64 (over x, z, core), head: 8 (over y).
Axes of the slice: x: 4, y: 8, z: 8, core: 2. Of those that a mesh axis runs over, the one named last changes fastest.
Arguments:
- queries: bfloat16 [49152, 1024], P('seq', 'head'), may hold values from -5 to 5
- key_rows: bfloat16 [49152, 1024], P('seq', 'head'), may hold values from -5 to 5
- values: bfloat16 [49152, 1024], P('seq', 'head'), may hold values from -6 to 6
- offsets: int32 [4, 8], replicated, may hold values from 0 to 7, as said below
Outputs:
- attended: bfloat16 [49152, 1024], P(('seq', 'head'))
The draws below stay inside these ranges and needn't reach their ends.
Inputs may be any that keep to these rules, and one draw needn't show every extreme that they name: offsets[b, h] lies in 0 to 2**b - 1, and in every branch b some head has offset 2**b - 1.
All inputs are finite; a program needn't handle non-finite values.
Results may differ from the reference program's by a relative error of at most 0.0045.
Values may be sent and summed in bfloat16 or wider, within the bound.
No kernel may reach another device: no remote copies, remote signals or barrier semaphores. Data moves between devices by JAX's collectives and lax.ppermute only.
A program may use at most 128 MiB of HBM per device.

```python
import math
import jax
import jax.numpy as jnp
from jax import lax

HD = 128
HEADS = 8
NB = 4
TOKENS = 49152
SEG_ROWS = 6144


def draw_queries(key, part):
    key = jax.random.fold_in(key, 11)
    base = jnp.clip(1.5 * jax.random.normal(key, (TOKENS, HEADS * HD), jnp.float32), -5.0, 5.0)
    return base.astype(jnp.bfloat16)


def draw_key_rows(key, part):
    key = jax.random.fold_in(key, 12)
    base = jnp.clip(1.5 * jax.random.normal(key, (TOKENS, HEADS * HD), jnp.float32), -5.0, 5.0)
    return base.astype(jnp.bfloat16)


def draw_offsets(key, part):
    key = jax.random.fold_in(key, 13)
    limits = 2 ** jnp.arange(NB, dtype=jnp.int32)
    drawn = jax.random.randint(key, (NB, HEADS), 0, limits[:, None], dtype=jnp.int32)
    forced_head = jax.random.randint(jax.random.fold_in(key, 1), (NB,), 0, HEADS, dtype=jnp.int32)
    columns = jnp.arange(HEADS, dtype=jnp.int32)
    return jnp.where(columns[None, :] == forced_head[:, None], limits[:, None] - 1, drawn)


def shard_levels(key, shape, split, least, top_value):
    level = 1.0
    for dim, blocks in split:
        heights = jax.random.uniform(jax.random.fold_in(jax.random.fold_in(key, 6), dim), (blocks,), jnp.float32, least / len(split), top_value / len(split))
        level = level * jnp.repeat(jnp.exp(heights), shape[dim] // blocks).reshape((-1,) + (1,) * (len(shape) - 1 - dim))
    return level


def scatter_about(rng, extent, deviation, reach, split=(), kind=jnp.bfloat16):
    entries = deviation * jax.random.normal(rng, extent, jnp.float32)
    if split:
        entries = entries * shard_levels(rng, extent, split, -0.22, 0.18)
    return jnp.clip(entries, -reach, reach).astype(kind)


def setup_inputs(seed: int = 0) -> dict:
    key_of = jax.random.split(jax.random.key(seed), 5)
    return {
        "queries": draw_queries(jax.random.fold_in(key_of[4], 71), 0),
        "key_rows": draw_key_rows(jax.random.fold_in(key_of[4], 71), 0),
        "values": scatter_about(key_of[2], (TOKENS, HEADS * HD), 1.0, 6.0, ((0, 64), (1, 8))),
        "offsets": draw_offsets(jax.random.fold_in(key_of[4], 71), 0),
    }


def attend_segment(operands):
    seg_q, seg_k, seg_v = operands
    score_scale = 1.0 / math.sqrt(HD)
    scores = jnp.dot(seg_q, seg_k.T, preferred_element_type=jnp.float32) * score_scale
    positions = jnp.arange(SEG_ROWS, dtype=jnp.int32)
    causal = positions[:, None] >= positions[None, :]
    scores = jnp.where(causal, scores, -jnp.inf)
    row_max = lax.optimization_barrier(jnp.max(scores, axis=1))
    probs = jnp.exp(scores - row_max[:, None])
    row_sum = lax.optimization_barrier(jnp.sum(probs, axis=1))
    mixed = jnp.dot(probs.astype(jnp.bfloat16), seg_v, preferred_element_type=jnp.float32)
    return (mixed / row_sum[:, None], row_max + jnp.log(row_sum))

def branch_head(q_head, k_head, v_head, head_offset, dilation):
    selected_rows = TOKENS // dilation

    def pick_rows(source):
        grouped = source.reshape(selected_rows, dilation, HD)
        chosen = lax.dynamic_index_in_dim(grouped, head_offset, 1, keepdims=False)
        return chosen.reshape(selected_rows // SEG_ROWS, SEG_ROWS, HD)
    branch_out, log_total = lax.map(attend_segment, (pick_rows(q_head), pick_rows(k_head), pick_rows(v_head)))
    onehot = jnp.arange(dilation, dtype=jnp.int32) == head_offset
    full_out = branch_out.reshape(selected_rows, 1, HD) * onehot[None, :, None].astype(jnp.float32)
    full_log = jnp.broadcast_to(log_total.reshape(selected_rows, 1), (selected_rows, dilation))
    picked = jnp.broadcast_to(onehot[None, :], (selected_rows, dilation))
    return (full_out.reshape(TOKENS, HD), full_log.reshape(TOKENS), picked.reshape(TOKENS))

def reference(queries, key_rows, values, offsets):
    head_outputs = []
    for head in range(HEADS):
        q_head = queries[:, head * HD:(head + 1) * HD]
        k_head = key_rows[:, head * HD:(head + 1) * HD]
        v_head = values[:, head * HD:(head + 1) * HD]
        outs_list, logs_list, picks_list = ([], [], [])
        for branch in range(NB):
            full_out, full_log, picked = branch_head(q_head, k_head, v_head, offsets[branch, head], 2 ** branch)
            outs_list.append(full_out)
            logs_list.append(full_log)
            picks_list.append(picked)
        branch_outs = jnp.stack(outs_list)
        branch_logs = jnp.stack(logs_list)
        branch_picks = jnp.stack(picks_list)
        best_log = lax.optimization_barrier(jnp.max(jnp.where(branch_picks, branch_logs, -jnp.inf), axis=0))
        merge_weight = jnp.where(branch_picks, jnp.exp(branch_logs - best_log[None]), 0.0)
        merged = lax.optimization_barrier(jnp.sum(merge_weight[:, :, None] * branch_outs, axis=0)) / lax.optimization_barrier(jnp.sum(merge_weight, axis=0))[:, None]
        head_outputs.append(merged)
    return jnp.concatenate(head_outputs, axis=1).astype(jnp.bfloat16)
```

```python
import math

import jax
import jax.numpy as jnp
from jax import lax
from jax.experimental import pallas as pl
from jax.experimental.pallas import tpu as pltpu
from jax.sharding import PartitionSpec as P

ROWS = 768
HD = 128
CHUNK = 256
LANES = 8
GROUPS = 8
BRANCHES = 4
PICKED = (0, 384, 192, 96)
START = (0, 0, 384, 576)
TOTAL = 672
CUT = (0, 0, 384, 384, 576, 576, 576, 576)
SCALE = math.log2(math.e) / math.sqrt(HD)
NEG = -1e30
LOW, HIGH = 2.0**-60, 2.0**120
F32, BF16 = jnp.float32, jnp.bfloat16


def message_rows(d):
    rows = TOTAL - CUT[d]
    sums = -(-rows // 128)
    return rows, sums, rows + -(-3 * sums // 16) * 16


def iota(shape, axis):
    return lax.broadcasted_iota(jnp.int32, shape, axis)


def dot_t(a, b):
    return lax.dot_general(a, b, (((1,), (1,)), ((), ())), preferred_element_type=F32)


def pick_matrix(sm):
    parts = []
    for b in range(1, BRANCHES):
        count, dilation = CHUNK >> b, 1 << b
        hit = iota((count, CHUNK), 1) == iota((count, CHUNK), 0) * dilation + sm[1 + b]
        parts.append(jnp.where(hit, 1.0, 0.0).astype(BF16))
    return jnp.concatenate(parts, axis=0)


def with_ones(values):
    return jnp.concatenate([values, jnp.ones_like(values)], axis=1)


def prep_kernel(sm, q, k, v, kv, near, middle, far):
    kv[:, :HD] = k[...]
    kv[:, HD:] = v[...]
    pick = pick_matrix(sm)
    for c in range(ROWS // CHUNK):
        got = jnp.dot(pick, q[c * CHUNK : (c + 1) * CHUNK, :], preferred_element_type=F32).astype(BF16)
        for b in range(1, BRANCHES):
            count = CHUNK >> b
            at = CHUNK - (CHUNK >> (b - 1))
            piece = got[at : at + count, :]
            row = START[b] + c * count
            near[row : row + count, :] = piece
            if b >= 2:
                middle[row - 384 : row - 384 + count, :] = piece
            if b >= 3:
                far[row - 576 : row - 576 + count, :] = piece


def fast_tile(q, kv, allowed=None):
    p = jnp.exp2(dot_t(q, kv[:, :HD]) * SCALE)
    if allowed is not None:
        p = jnp.where(allowed, p, 0.0)
    return jnp.dot(p.astype(BF16), with_ones(kv[:, HD:]), preferred_element_type=F32)


def slow_tile(q, kv, allowed, acc, top, rows):
    s = jnp.where(allowed, dot_t(q, kv[:, :HD]) * SCALE, NEG)
    old = top[rows, :]
    new = jnp.maximum(old, jnp.broadcast_to(jnp.max(s, axis=1, keepdims=True), old.shape))
    factor = jnp.exp2(old - new)
    p = jnp.where(allowed, jnp.exp2(s - new[:, :1]), 0.0).astype(BF16)
    added = jnp.dot(p, with_ones(kv[:, HD:]), preferred_element_type=F32)
    acc[rows, :] = acc[rows, :] * jnp.concatenate([factor, factor], axis=1) + added
    top[rows, :] = new


def in_range(total):
    return (jnp.min(total) >= LOW) & (jnp.max(total) <= HIGH)


def branch_pass(q, kv, acc, top, own, lane):
    keys = kv.shape[0]
    step = 768
    acc[...] = jnp.zeros_like(acc)
    top[...] = jnp.zeros_like(top)

    def fast(i, carry):
        block = kv[pl.ds(pl.multiple_of(i * step, step), step), :]
        for c in range(ROWS // CHUNK):
            rows = pl.ds(c * CHUNK, CHUNK)
            allowed = None
            if c * CHUNK < own:
                row = iota((CHUNK, step), 0) + c * CHUNK
                col = iota((CHUNK, step), 1) + i * step
                allowed = (row >= own) | (col <= row + lane * own)
            acc[rows, :] += fast_tile(q[rows, :], block, allowed)
        return carry

    lax.fori_loop(0, keys // step, fast, 0)

    @pl.when(jnp.logical_not(in_range(acc[:, HD:])))
    def _():
        acc[...] = jnp.zeros_like(acc)
        top[...] = jnp.full_like(top, NEG)

        def slow(i, carry):
            block = kv[pl.ds(pl.multiple_of(i * CHUNK, CHUNK), CHUNK), :]

            def rows_step(c, inner):
                rows = pl.ds(pl.multiple_of(c * CHUNK, CHUNK), CHUNK)
                row = iota((CHUNK, CHUNK), 0) + c * CHUNK
                col = iota((CHUNK, CHUNK), 1) + i * CHUNK
                allowed = (row >= own) | (col <= row + lane * own)
                slow_tile(q[rows, :], block, allowed, acc, top, rows)
                return inner

            return lax.fori_loop(0, ROWS // CHUNK, rows_step, carry)

        lax.fori_loop(0, keys // CHUNK, slow, 0)


def split3(x):
    high = x.astype(BF16)
    rest = x - high.astype(F32)
    mid = rest.astype(BF16)
    return high, mid, (rest - mid.astype(F32)).astype(BF16)


def block_index(r, sibling, lane):
    z, core = lane // 2, lane % 2
    return lax.rem(z - r + 4, 4) * 2 + (1 - core if sibling else core)


def cross_kernel(sm, *refs):
    kvs, refs = refs[:8], refs[8:]
    own_q, refs = refs[0], refs[1:]
    qs, refs = (None,) + refs[:7], refs[7:]
    outs, refs = (None,) + refs[:7], refs[7:]
    own_out, own_sum, refs = refs[0], refs[1], refs[2:]
    keys, refs = (None,) + refs[:3], refs[3:]
    q_all, acc, top, sums = refs[0], refs[1], refs[2], (None,) + refs[3:10]
    lane = sm[1]
    pick = pick_matrix(sm)
    for n, kv in enumerate(kvs):
        block = block_index(n // 2, n % 2, lane)
        for c in range(ROWS // CHUNK):
            got = jnp.dot(pick, kv[c * CHUNK : (c + 1) * CHUNK, :], preferred_element_type=F32).astype(BF16)
            for b in range(1, BRANCHES):
                count = CHUNK >> b
                at = CHUNK - (CHUNK >> (b - 1))
                row = pl.multiple_of(block * PICKED[b] + c * count, count)
                keys[b][pl.ds(row, count), :] = got[at : at + count, :]
    for d in range(1, GROUPS):
        sums[d][...] = jnp.zeros_like(sums[d])
    for b in range(1, BRANCHES):
        own, first = PICKED[b], START[b]
        q_all[0:own, :] = own_q[first : first + own, :]
        for d in range(1, 1 << b):
            q_all[d * own : (d + 1) * own, :] = qs[d][first - CUT[d] : first - CUT[d] + own, :]
        branch_pass(q_all, keys[b], acc, top, own, lane)
        for d in range(1 << b):
            rows = slice(d * own, (d + 1) * own)
            total = acc[rows, HD:]
            out = acc[rows, :HD] / total
            log_sum = top[rows, :] + jnp.log2(total)
            if d == 0:
                own_out[first : first + own, :] = out
                own_sum[first : first + own, :] = log_sum
            else:
                at = first - CUT[d]
                outs[d][at : at + own, :] = out.astype(BF16)
                sums[d][at : at + own, :] = log_sum
    diagonal = iota((128, 128), 0) == iota((128, 128), 1)
    for d in range(1, GROUPS):
        rows, count, padded = message_rows(d)
        tail = jnp.zeros((padded - rows, 128), F32)
        place = iota(tail.shape, 0)
        for c in range(count):
            line = jnp.sum(jnp.where(diagonal, sums[d][c * 128 : (c + 1) * 128, :], 0.0), axis=0, keepdims=True)
            for n, piece in enumerate(split3(line)):
                tail = jnp.where(place == 3 * c + n, jnp.broadcast_to(piece.astype(F32), tail.shape), tail)
        outs[d][rows:padded, :] = tail.astype(BF16)


def dense_kernel(sm, *refs):
    kvs = refs[:8]
    q, out, log_sum, acc, top = refs[8:]
    lane = sm[1]
    top[...] = jnp.zeros_like(top)
    lower = iota((CHUNK, CHUNK), 1) <= iota((CHUNK, CHUNK), 0)
    for c in range(ROWS // CHUNK):
        rows = pl.ds(c * CHUNK, CHUNK)
        total = fast_tile(q[rows, :], kvs[0][c * CHUNK : (c + 1) * CHUNK, :], lower)
        if c:
            total = total + fast_tile(q[rows, :], kvs[0][: c * CHUNK, :])
        acc[rows, :] = total
    for n in range(1, 8):

        @pl.when(block_index(n // 2, n % 2, lane) < lane)
        def _(n=n):
            for c in range(ROWS // CHUNK):
                rows = pl.ds(c * CHUNK, CHUNK)
                acc[rows, :] += fast_tile(q[rows, :], kvs[n][...])

    @pl.when(jnp.logical_not(in_range(acc[:, HD:])))
    def _():
        acc[...] = jnp.zeros_like(acc)
        top[...] = jnp.full_like(top, NEG)
        for n in range(8):
            block = block_index(n // 2, n % 2, lane)

            @pl.when(block <= lane)
            def _(n=n, block=block):
                def step(i, carry):
                    c, k = i // 3, lax.rem(i, 3)
                    rows = pl.ds(pl.multiple_of(c * CHUNK, CHUNK), CHUNK)
                    part = kvs[n][pl.ds(pl.multiple_of(k * CHUNK, CHUNK), CHUNK), :]
                    row = iota((CHUNK, CHUNK), 0) + c * CHUNK + lane * ROWS
                    col = iota((CHUNK, CHUNK), 1) + k * CHUNK + block * ROWS
                    slow_tile(q[rows, :], part, col <= row, acc, top, rows)
                    return carry

                lax.fori_loop(0, 9, step, 0)

    total = acc[:, HD:]
    out[...] = acc[:, :HD] / total
    log_sum[...] = top[...] + jnp.log2(total)


def merge_kernel(sm, *refs):
    got, refs = (None,) + refs[:7], refs[7:]
    own_out, own_sum, out0, sum0, merged, got_sums = refs[0], refs[1], refs[2], refs[3], refs[4], (None,) + refs[5:12]
    compact, compact_sum = refs[12], refs[13]
    group = sm[0]
    diagonal = iota((128, 128), 0) == iota((128, 128), 1)
    ones = jnp.ones((128, 128), BF16)
    for d in range(1, GROUPS):
        rows, count, _ = message_rows(d)
        for c in range(count):
            total = jnp.zeros((128, 128), F32)
            for n in range(3):
                line = got[d][rows + 3 * c + n : rows + 3 * c + n + 1, :]
                spread = jnp.where(diagonal, jnp.broadcast_to(line.astype(F32), (128, 128)), 0.0).astype(BF16)
                total = total + jnp.dot(spread, ones, preferred_element_type=F32)
            got_sums[d][c * 128 : (c + 1) * 128, :] = total
    for b in range(1, BRANCHES):
        own, first = PICKED[b], START[b]
        outs = [own_out[first : first + own, :]]
        logs = [own_sum[first : first + own, :]]
        for d in range(1, 1 << b):
            at = first - CUT[d]
            valid = lax.rem(group, 1 << b) >= d
            outs.append(got[d][at : at + own, :].astype(F32))
            logs.append(jnp.where(valid, got_sums[d][at : at + own, :], NEG))
        best = logs[0]
        for log in logs[1:]:
            best = jnp.maximum(best, log)
        top = jnp.zeros_like(best)
        bottom = jnp.zeros_like(best)
        for out, log in zip(outs, logs):
            weight = jnp.exp2(log - best)
            top = top + weight * out
            bottom = bottom + weight
        compact[first : first + own, :] = top / bottom
        compact_sum[first : first + own, :] = best + jnp.log2(bottom)
    for c in range(ROWS // CHUNK):
        rows = slice(c * CHUNK, (c + 1) * CHUNK)
        outs = [out0[rows, :]]
        logs = [sum0[rows, :]]
        for b in range(1, BRANCHES):
            count, dilation = CHUNK >> b, 1 << b
            at = START[b] + c * count
            offset = sm[1 + b]
            place = jnp.where(
                iota((CHUNK, count), 0) == iota((CHUNK, count), 1) * dilation + offset, 1.0, 0.0
            ).astype(BF16)
            out_parts = split3(compact[at : at + count, :])
            log_parts = split3(compact_sum[at : at + count, :])
            first = jnp.concatenate([out_parts[0], log_parts[0]], axis=1)
            second = jnp.concatenate([out_parts[1], log_parts[1]], axis=1)
            spread = jnp.dot(place, first, preferred_element_type=F32)
            spread = spread + jnp.dot(place, second, preferred_element_type=F32)
            log = spread[:, HD:] + jnp.dot(place, log_parts[2], preferred_element_type=F32)
            chosen = lax.rem(iota((CHUNK, HD), 0), dilation) == offset
            outs.append(spread[:, :HD])
            logs.append(jnp.where(chosen, log, NEG))
        best = logs[0]
        for log in logs[1:]:
            best = jnp.maximum(best, log)
        top = jnp.zeros_like(best)
        bottom = jnp.zeros_like(best)
        for out, log in zip(outs, logs):
            weight = jnp.exp2(log - best)
            top = top + weight * out
            bottom = bottom + weight
        merged[rows, :] = (top / bottom).astype(BF16)


def call(kernel, name, sm, operands, outputs, scratch, flops):
    shapes = [jax.ShapeDtypeStruct(shape, dtype) for shape, dtype in outputs]
    moved = sum(math.prod(x.shape) * x.dtype.itemsize for x in list(operands) + shapes)
    return pl.pallas_call(
        kernel,
        name=name,
        out_shape=shapes,
        in_specs=[pl.BlockSpec(memory_space=pltpu.SMEM)]
        + [pl.BlockSpec(memory_space=pltpu.VMEM)] * len(operands),
        out_specs=[pl.BlockSpec(memory_space=pltpu.VMEM)] * len(shapes),
        scratch_shapes=[pltpu.VMEM(shape, dtype) for shape, dtype in scratch],
        compiler_params=pltpu.CompilerParams(vmem_limit_bytes=48 * 1024 * 1024),
        cost_estimate=pl.CostEstimate(flops=flops, bytes_accessed=moved, transcendentals=0),
    )(sm, *operands)


def place_of(index):
    x, z, core = index // 16, index // 2 % 8, index % 2
    return 2 * x + z // 4, z % 4, core


def index_of(group, z, core):
    return (group // 2 * 8 + group % 2 * 4 + z) * 2 + core


def to_earlier(d):
    pairs = []
    for index in range(64):
        group, z, core = place_of(index)
        if group >= d:
            pairs.append((index, index_of(group - d, z ^ 2 if d % 2 else z, core)))
    return pairs


def rotation(r):
    pairs = []
    for index in range(64):
        group, z, core = place_of(index)
        pairs.append((index, index_of(group, (z + r) % 4, core)))
    return pairs


def on_device(queries, key_rows, values, offsets):
    seq, head = lax.axis_index("seq"), lax.axis_index("head")
    mine = lax.dynamic_slice_in_dim(offsets, head, 1, axis=1)[:, 0]
    sm = jnp.concatenate([jnp.stack([seq // 8, seq % 8]).astype(jnp.int32), mine[1:], jnp.zeros((3,), jnp.int32)])
    kv, near, middle, far = call(
        prep_kernel,
        "pick_queries",
        sm,
        [queries, key_rows, values],
        [((ROWS, 2 * HD), BF16), ((TOTAL, HD), BF16), ((288, HD), BF16), ((96, HD), BF16)],
        [],
        2 * 672 * 256 * 128,
    )
    pair = [(i, i ^ 1) for i in range(64)]
    gathered = [kv] + [lax.ppermute(kv, "seq", rotation(r)) for r in (1, 2, 3)]
    kvs = []
    for block in gathered:
        kvs += [block, lax.ppermute(block, "seq", pair)]
    sent = [None, near, middle, middle, far, far, far, far]
    visiting = [lax.ppermute(sent[d], "seq", to_earlier(d)) for d in range(1, GROUPS)]
    crossed = call(
        cross_kernel,
        "branches_1_to_3",
        sm,
        kvs + [near] + visiting,
        [((message_rows(d)[2], HD), BF16) for d in range(1, GROUPS)] + [((TOTAL, HD), F32)] * 2,
        [((3072, 2 * HD), BF16), ((1536, 2 * HD), BF16), ((768, 2 * HD), BF16)]
        + [((ROWS, HD), BF16), ((ROWS, 2 * HD), F32), ((ROWS, HD), F32)]
        + [((message_rows(d)[1] * 128, 128), F32) for d in range(1, GROUPS)],
        4 * 768 * 5376 * 128,
    )
    back = [
        lax.ppermute(crossed[d - 1], "seq", [(b, a) for a, b in to_earlier(d)]) for d in range(1, GROUPS)
    ]
    out0, sum0 = call(
        dense_kernel,
        "branch_0",
        sm,
        kvs + [queries],
        [((ROWS, HD), F32)] * 2,
        [((ROWS, 2 * HD), F32), ((ROWS, HD), F32)],
        4 * 768 * 6144 * 128,
    )
    (merged,) = call(
        merge_kernel,
        "merge",
        sm,
        back + list(crossed[7:]) + [out0, sum0],
        [((ROWS, HD), BF16)],
        [((message_rows(d)[1] * 128, 128), F32) for d in range(1, GROUPS)] + [((TOTAL, HD), F32)] * 2,
        1000000,
    )
    return lax.all_to_all(merged, "head", split_axis=0, concat_axis=1, tiled=True)


def solution(mesh):
    placed = (P("seq", "head"), P("seq", "head"), P("seq", "head"), P())
    return jax.shard_map(
        on_device, mesh=mesh, in_specs=placed, out_specs=P(("seq", "head"), None), check_vma=False
    )
```

```python
import functools
import math

import jax
import jax.numpy as jnp
from jax import lax
from jax.experimental import pallas as pl
from jax.experimental.pallas import tpu as pltpu
from jax.sharding import PartitionSpec as P

ROWS = 768
HD = 128
CHUNK = 256
LANES = 8
GROUPS = 8
BRANCHES = 4
PICKED = (0, 384, 192, 96)
START = (0, 0, 384, 576)
TOTAL = 672
CROSS = (0, 384, 576, 672)
CROSS_START = (0, 0, 384, 960)
VISITING = 1632
CUT = (0, 0, 384, 384, 576, 576, 576, 576)
SCALE = math.log2(math.e) / math.sqrt(HD)
NEG = -1e30
LOW, HIGH = 2.0**-60, 2.0**120
F32, BF16 = jnp.float32, jnp.bfloat16


def message_rows(d):
    rows = TOTAL - CUT[d]
    sums = -(-rows // 128)
    return rows, sums, rows + -(-3 * sums // 16) * 16


def iota(shape, axis):
    return lax.broadcasted_iota(jnp.int32, shape, axis)


def dot_t(a, b):
    return lax.dot_general(a, b, (((1,), (1,)), ((), ())), preferred_element_type=F32)


def pick_matrix(sm):
    parts = []
    for b in range(1, BRANCHES):
        count, dilation = CHUNK >> b, 1 << b
        hit = iota((count, CHUNK), 1) == iota((count, CHUNK), 0) * dilation + sm[1 + b]
        parts.append(jnp.where(hit, 1.0, 0.0).astype(BF16))
    return jnp.concatenate(parts, axis=0)


def with_ones(values):
    return jnp.concatenate([values, jnp.ones_like(values)], axis=1)


def split3(x):
    high = x.astype(BF16)
    rest = x - high.astype(F32)
    mid = rest.astype(BF16)
    return high, mid, (rest - mid.astype(F32)).astype(BF16)


def pack_kernel(k, v, kv, sems):
    copies = [
        pltpu.make_async_copy(k, kv.at[:, pl.ds(0, HD)], sems.at[0]),
        pltpu.make_async_copy(v, kv.at[:, pl.ds(HD, HD)], sems.at[1]),
    ]
    for copy in copies:
        copy.start()
    for copy in copies:
        copy.wait()


def pick_kernel(sm, q, near):
    pick = pick_matrix(sm)
    for c in range(ROWS // CHUNK):
        got = jnp.dot(pick, q[c * CHUNK : (c + 1) * CHUNK, :], preferred_element_type=F32).astype(BF16)
        for b in range(1, BRANCHES):
            count = CHUNK >> b
            at = CHUNK - (CHUNK >> (b - 1))
            piece = got[at : at + count, :]
            row = START[b] + c * count
            near[row : row + count, :] = piece


def fast_tile(q, kv, allowed=None):
    p = jnp.exp2(dot_t(q, kv[:, :HD]) * SCALE)
    if allowed is not None:
        p = jnp.where(allowed, p, 0.0)
    return jnp.dot(p.astype(BF16), with_ones(kv[:, HD:]), preferred_element_type=F32)


def slow_tile(q, kv, allowed, acc, top, rows):
    s = dot_t(q, kv[:, :HD]) * SCALE
    if allowed is not None:
        s = jnp.where(allowed, s, NEG)
    old = top[rows, :]
    new = jnp.maximum(old, jnp.broadcast_to(jnp.max(s, axis=1, keepdims=True), old.shape))
    factor = jnp.exp2(old - new)
    p = jnp.exp2(s - new[:, :1])
    if allowed is not None:
        p = jnp.where(allowed, p, 0.0)
    added = jnp.dot(p.astype(BF16), with_ones(kv[:, HD:]), preferred_element_type=F32)
    acc[rows, :] = acc[rows, :] * jnp.concatenate([factor, factor], axis=1) + added
    top[rows, :] = new


def in_range(total):
    return (jnp.min(total) >= LOW) & (jnp.max(total) <= HIGH)


def select_keys(sm, kv, keys, part):
    pick = pick_matrix(sm)
    for c in range(ROWS // CHUNK):
        got = jnp.dot(pick, kv[c * CHUNK : (c + 1) * CHUNK, :], preferred_element_type=F32).astype(BF16)
        for b in range(1, BRANCHES):
            count = CHUNK >> b
            at = CHUNK - (CHUNK >> (b - 1))
            row = part * PICKED[b] + c * count
            keys[b][row : row + count, :] = got[at : at + count, :]


def add_cross(q, keys, acc, first):
    for b in range(1, BRANCHES):
        size = CROSS[b]
        step = 192
        for at in range(0, size, step):
            rows = pl.ds(CROSS_START[b] + at, min(step, size - at))
            total = fast_tile(q[rows, :], keys[b][...])
            acc[rows, :] = total if first else acc[rows, :] + total


def add_own(q, own_q, blocks, keys, acc):
    for c in range(ROWS // CHUNK):
        rows = pl.ds(c * CHUNK, CHUNK)
        total = acc[rows, :]
        for kv in blocks:
            total = total + fast_tile(q[rows, :], kv[...])
        acc[rows, :] = total
    for b in range(1, BRANCHES):
        step = min(192, PICKED[b])
        for at in range(0, PICKED[b], step):
            start = START[b] + at
            rows = pl.ds(ROWS + start, step)
            acc[rows, :] += fast_tile(own_q[start : start + step, :], keys[b][...])


def first_kernel(sm, mine, other, q, near, own, *keys):
    keys = (None,) + keys
    select_keys(sm, mine, keys, 0)
    select_keys(sm, other, keys, 1)
    lower = iota((CHUNK, CHUNK), 1) <= iota((CHUNK, CHUNK), 0)
    for c in range(ROWS // CHUNK):
        rows = pl.ds(c * CHUNK, CHUNK)
        total = fast_tile(q[rows, :], mine[c * CHUNK : (c + 1) * CHUNK, :], lower)
        if c:
            total = total + fast_tile(q[rows, :], mine[: c * CHUNK, :])
        own[rows, :] = total
    for b in range(1, BRANCHES):
        size = PICKED[b]
        lower = iota((size, size), 1) <= iota((size, size), 0)
        own[ROWS + START[b] : ROWS + START[b] + size, :] = fast_tile(
            near[START[b] : START[b] + size, :], keys[b][0:size, :], lower
        )

    @pl.when(lax.rem(sm[1], 2) == 1)
    def _():
        for c in range(ROWS // CHUNK):
            rows = pl.ds(c * CHUNK, CHUNK)
            own[rows, :] += fast_tile(q[rows, :], other[...])
        for b in range(1, BRANCHES):
            size = PICKED[b]
            rows = pl.ds(ROWS + START[b], size)
            own[rows, :] += fast_tile(near[START[b] : START[b] + size, :], keys[b][size : 2 * size, :])


def second_kernel(sm, mine0, other0, mine, other, q, near, r1, r2, r4, r6, own_in, visiting, cross, own, *keys):
    del own_in
    keys = (None,) + keys
    visiting[0:384, :] = r1[0:384, :]
    visiting[384:576, :] = r1[384:576, :]
    visiting[576:768, :] = r2[0:192, :]
    visiting[768:960, :] = r2[288:480, :]
    visiting[960:1056, :] = r1[576:672, :]
    visiting[1056:1152, :] = r2[192:288, :]
    visiting[1152:1248, :] = r2[480:576, :]
    visiting[1248:1440, :] = r4[...]
    visiting[1440:1632, :] = r6[...]
    select_keys(sm, mine0, keys, 0)
    select_keys(sm, other0, keys, 1)
    add_cross(visiting, keys, cross, True)
    select_keys(sm, mine, keys, 0)
    select_keys(sm, other, keys, 1)
    add_cross(visiting, keys, cross, False)

    @pl.when(before(sm, 1))
    def _():
        add_own(q, near, (mine, other), keys, own)


def before(sm, stage):
    z = sm[1] // 2
    return jnp.bitwise_xor(z, stage) < z


def stage_kernel(stage, sm, mine, other, q, near, visiting, cross_in, own_in, cross, own, *keys):
    del cross_in, own_in
    keys = (None,) + keys
    select_keys(sm, mine, keys, 0)
    select_keys(sm, other, keys, 1)
    add_cross(visiting, keys, cross, False)

    @pl.when(before(sm, stage))
    def _():
        add_own(q, near, (mine, other), keys, own)


def last_cross_kernel(sm, *refs):
    kvs, refs = refs[:8], refs[8:]
    visiting, cross, refs = refs[0], refs[2], refs[3:]
    outs, refs = (None,) + refs[:7], refs[7:]
    keys, top, sums = (None,) + refs[:3], refs[3], (None,) + refs[4:11]
    select_keys(sm, kvs[6], keys, 0)
    select_keys(sm, kvs[7], keys, 1)
    add_cross(visiting, keys, cross, False)
    top[...] = jnp.zeros_like(top)

    @pl.when(jnp.logical_not(in_range(cross[:, HD:])))
    def _():
        cross[...] = jnp.zeros_like(cross)
        top[...] = jnp.full_like(top, NEG)
        for n in range(0, 8, 2):
            select_keys(sm, kvs[n], keys, 0)
            select_keys(sm, kvs[n + 1], keys, 1)
            for b in range(1, BRANCHES):

                def step(i, carry, b=b):
                    rows = pl.ds(pl.multiple_of(CROSS_START[b] + i * 96, 96), 96)
                    slow_tile(visiting[rows, :], keys[b], None, cross, top, rows)
                    return carry

                lax.fori_loop(0, CROSS[b] // 96, step, 0)

    for d in range(1, GROUPS):
        sums[d][...] = jnp.zeros_like(sums[d])
    for b in range(1, BRANCHES):
        for d in range(1, 1 << b):
            row = CROSS_START[b] + (d - 1) * PICKED[b]
            rows = slice(row, row + PICKED[b])
            total = cross[rows, HD:]
            at = START[b] - CUT[d]
            outs[d][at : at + PICKED[b], :] = (cross[rows, :HD] / total).astype(BF16)
            sums[d][at : at + PICKED[b], :] = top[rows, :] + jnp.log2(total)
    diagonal = iota((128, 128), 0) == iota((128, 128), 1)
    for d in range(1, GROUPS):
        rows, count, padded = message_rows(d)
        tail = jnp.zeros((padded - rows, 128), F32)
        place = iota(tail.shape, 0)
        for c in range(count):
            line = jnp.sum(jnp.where(diagonal, sums[d][c * 128 : (c + 1) * 128, :], 0.0), axis=0, keepdims=True)
            for n, piece in enumerate(split3(line)):
                tail = jnp.where(place == 3 * c + n, jnp.broadcast_to(piece.astype(F32), tail.shape), tail)
        outs[d][rows:padded, :] = tail.astype(BF16)


def last_own_kernel(sm, *refs):
    kvs, refs = refs[:8], refs[8:]
    q, near, own, out, log_sum, refs = refs[0], refs[1], refs[3], refs[4], refs[5], refs[6:]
    keys, top = (None,) + refs[:3], refs[3]
    lane = sm[1]

    @pl.when(before(sm, 3))
    def _():
        select_keys(sm, kvs[6], keys, 0)
        select_keys(sm, kvs[7], keys, 1)
        add_own(q, near, kvs[6:8], keys, own)

    top[...] = jnp.zeros_like(top)

    @pl.when(jnp.logical_not(in_range(own[:, HD:])))
    def _():
        own[...] = jnp.zeros_like(own)
        top[...] = jnp.full_like(top, NEG)
        for n in range(8):
            z = jnp.bitwise_xor(lane // 2, n // 2)
            block = 2 * z + (lax.rem(lane, 2) if n % 2 == 0 else 1 - lax.rem(lane, 2))

            @pl.when(block <= lane)
            def _(n=n, block=block):
                select_keys(sm, kvs[n], keys, 0)
                for b in range(BRANCHES):
                    size = ROWS >> b
                    source, key = (q, kvs[n]) if b == 0 else (near, keys[b])

                    def step(i, carry, b=b, size=size, source=source, key=key):
                        at = pl.multiple_of(START[b] + i * 96, 96)
                        rows = pl.ds(pl.multiple_of((ROWS if b else 0) + at, 96), 96)
                        row = iota((96, size), 0) + i * 96 + lane * size
                        col = iota((96, size), 1) + block * size
                        slow_tile(source[pl.ds(at, 96), :], key[0:size, :], col <= row, own, top, rows)
                        return carry

                    lax.fori_loop(0, size // 96, step, 0)

    total = own[:, HD:]
    out[...] = own[:, :HD] / total
    log_sum[...] = top[...] + jnp.log2(total)


def merge_kernel(sm, *refs):
    got, refs = (None,) + refs[:7], refs[7:]
    own_out, own_sum, merged, got_sums = refs[0], refs[1], refs[2], (None,) + refs[3:10]
    compact, compact_sum = refs[10], refs[11]
    group = sm[0]
    diagonal = iota((128, 128), 0) == iota((128, 128), 1)
    ones = jnp.ones((128, 128), BF16)
    for d in range(1, GROUPS):
        rows, count, _ = message_rows(d)
        for c in range(count):
            total = jnp.zeros((128, 128), F32)
            for n in range(3):
                line = got[d][rows + 3 * c + n : rows + 3 * c + n + 1, :]
                spread = jnp.where(diagonal, jnp.broadcast_to(line.astype(F32), (128, 128)), 0.0).astype(BF16)
                total = total + jnp.dot(spread, ones, preferred_element_type=F32)
            got_sums[d][c * 128 : (c + 1) * 128, :] = total
    for b in range(1, BRANCHES):
        own, first = PICKED[b], START[b]
        outs = [own_out[ROWS + first : ROWS + first + own, :]]
        logs = [own_sum[ROWS + first : ROWS + first + own, :]]
        for d in range(1, 1 << b):
            at = first - CUT[d]
            valid = jnp.bitwise_xor(group, d) < group
            outs.append(got[d][at : at + own, :].astype(F32))
            logs.append(jnp.where(valid, got_sums[d][at : at + own, :], NEG))
        best = logs[0]
        for log in logs[1:]:
            best = jnp.maximum(best, log)
        top = jnp.zeros_like(best)
        bottom = jnp.zeros_like(best)
        for out, log in zip(outs, logs):
            weight = jnp.exp2(log - best)
            top = top + weight * out
            bottom = bottom + weight
        compact[first : first + own, :] = top / bottom
        compact_sum[first : first + own, :] = best + jnp.log2(bottom)
    for c in range(ROWS // CHUNK):
        rows = slice(c * CHUNK, (c + 1) * CHUNK)
        outs = [own_out[rows, :]]
        logs = [own_sum[rows, :]]
        for b in range(1, BRANCHES):
            count, dilation = CHUNK >> b, 1 << b
            at = START[b] + c * count
            offset = sm[1 + b]
            place = jnp.where(
                iota((CHUNK, count), 0) == iota((CHUNK, count), 1) * dilation + offset, 1.0, 0.0
            ).astype(BF16)
            out_parts = split3(compact[at : at + count, :])
            log_parts = split3(compact_sum[at : at + count, :])
            first = jnp.concatenate([out_parts[0], log_parts[0]], axis=1)
            second = jnp.concatenate([out_parts[1], log_parts[1]], axis=1)
            spread = jnp.dot(place, first, preferred_element_type=F32)
            spread = spread + jnp.dot(place, second, preferred_element_type=F32)
            log = spread[:, HD:] + jnp.dot(place, log_parts[2], preferred_element_type=F32)
            chosen = lax.rem(iota((CHUNK, HD), 0), dilation) == offset
            outs.append(spread[:, :HD])
            logs.append(jnp.where(chosen, log, NEG))
        best = logs[0]
        for log in logs[1:]:
            best = jnp.maximum(best, log)
        top = jnp.zeros_like(best)
        bottom = jnp.zeros_like(best)
        for out, log in zip(outs, logs):
            weight = jnp.exp2(log - best)
            top = top + weight * out
            bottom = bottom + weight
        merged[rows, :] = (top / bottom).astype(BF16)


def call(kernel, name, sm, operands, outputs, scratch, flops, aliases=None):
    shapes = [jax.ShapeDtypeStruct(shape, dtype) for shape, dtype in outputs]
    moved = sum(math.prod(x.shape) * x.dtype.itemsize for x in list(operands) + shapes)
    return pl.pallas_call(
        kernel,
        name=name,
        out_shape=shapes,
        in_specs=[pl.BlockSpec(memory_space=pltpu.SMEM)]
        + [pl.BlockSpec(memory_space=pltpu.VMEM)] * len(operands),
        out_specs=[pl.BlockSpec(memory_space=pltpu.VMEM)] * len(shapes),
        scratch_shapes=[pltpu.VMEM(shape, dtype) for shape, dtype in scratch],
        input_output_aliases=aliases or {},
        compiler_params=pltpu.CompilerParams(vmem_limit_bytes=32 * 1024 * 1024),
        cost_estimate=pl.CostEstimate(flops=1, bytes_accessed=1, transcendentals=0),
    )(sm, *operands)


def pack(k, v):
    return pl.pallas_call(
        pack_kernel,
        name="pack",
        out_shape=jax.ShapeDtypeStruct((ROWS, 2 * HD), BF16),
        in_specs=[pl.BlockSpec(memory_space=pl.ANY)] * 2,
        out_specs=pl.BlockSpec(memory_space=pltpu.VMEM),
        scratch_shapes=[pltpu.SemaphoreType.DMA((2,))],
    )(k, v)


def place_of(index):
    x, z, core = index // 16, index // 2 % 8, index % 2
    return 2 * x + z // 4, z % 4, core


def index_of(group, z, core):
    return (group // 2 * 8 + group % 2 * 4 + z) * 2 + core


def partner(index, j):
    group, z, core = place_of(index)
    return index_of(group ^ j, z ^ 2 if j % 2 else z, core)


def meet(j):
    return [(index, partner(index, j)) for index in range(64)]


def to_later(j):
    return [(index, other) for index, other in meet(j) if place_of(other)[0] > place_of(index)[0]]


def exchange(step):
    pairs = []
    for index in range(64):
        group, z, core = place_of(index)
        pairs.append((index, index_of(group, z ^ step, core)))
    return pairs


def on_device(queries, key_rows, values, offsets):
    seq, head = lax.axis_index("seq"), lax.axis_index("head")
    mine = lax.dynamic_slice_in_dim(offsets, head, 1, axis=1)[:, 0]
    sm = jnp.concatenate([jnp.stack([seq // 8, seq % 8]).astype(jnp.int32), mine[1:], jnp.zeros((3,), jnp.int32)])
    kv = pack(key_rows, values)
    queries, kv = lax.optimization_barrier((queries, kv))
    (near,) = call(
        pick_kernel, "pick_queries", sm, [queries], [((TOTAL, HD), BF16)], [], 2 * 672 * 256 * 128
    )
    pair = [(i, i ^ 1) for i in range(64)]
    keys = [((ROWS, 2 * HD), BF16), ((384, 2 * HD), BF16), ((192, 2 * HD), BF16)]
    state = [((VISITING, 2 * HD), F32), ((ROWS + TOTAL, 2 * HD), F32)]
    work = 4 * HD * 2 * ROWS * 2 * ROWS
    r1 = lax.ppermute(near, "seq", meet(1))
    block2 = lax.ppermute(kv, "seq", exchange(2))
    block1 = lax.ppermute(kv, "seq", exchange(1))
    kvs = [kv, lax.ppermute(kv, "seq", pair)]
    r2 = lax.ppermute(jnp.concatenate([near[384:], r1[384:]]), "seq", meet(2))
    (own,) = call(first_kernel, "own_chip", sm, kvs + [queries, near], state[1:], keys, work // 2)
    pair3 = jnp.concatenate([near[576:], r1[576:]])
    r4 = lax.ppermute(pair3, "seq", meet(4))
    r6 = lax.ppermute(pair3, "seq", meet(6))
    block2, r2, r4, r6, own = lax.optimization_barrier((block2, r2, r4, r6, own))
    block3 = lax.ppermute(block2, "seq", exchange(1))
    block1, own = lax.optimization_barrier((block1, own))
    kvs += [block1, lax.ppermute(block1, "seq", pair)]
    kvs += [block2, lax.ppermute(block2, "seq", pair)]
    kvs[5], own = lax.optimization_barrier((kvs[5], own))
    visiting, cross, own = call(
        second_kernel,
        "chip_1",
        sm,
        kvs[:4] + [queries, near, r1, r2, r4, r6, own],
        [((VISITING, HD), BF16)] + state,
        keys,
        work,
        {11: 2},
    )
    cross, own = call(
        functools.partial(stage_kernel, 2),
        "chip_2",
        sm,
        kvs[4:] + [queries, near, visiting, cross, own],
        state,
        keys,
        work,
        {6: 0, 7: 1},
    )
    block3, own = lax.optimization_barrier((block3, own))
    kvs += [block3, lax.ppermute(block3, "seq", pair)]
    crossed = call(
        last_cross_kernel,
        "cross_end",
        sm,
        kvs + [visiting, cross],
        state[:1] + [((message_rows(d)[2], HD), BF16) for d in range(1, GROUPS)],
        keys + [((VISITING, HD), F32)] + [((message_rows(d)[1] * 128, 128), F32) for d in range(1, GROUPS)],
        work // 2,
        {10: 0},
    )
    back = [
        lax.ppermute(crossed[d], "seq", to_later(d)) for d in range(1, GROUPS)
    ]
    _, out, log_sum = call(
        last_own_kernel,
        "own_end",
        sm,
        kvs + [queries, near, own],
        state[1:] + [((ROWS + TOTAL, HD), F32)] * 2,
        keys + [((ROWS + TOTAL, HD), F32)],
        work // 2,
        {11: 0},
    )
    (merged,) = call(
        merge_kernel,
        "merge",
        sm,
        back + [out, log_sum],
        [((ROWS, HD), BF16)],
        [((message_rows(d)[1] * 128, 128), F32) for d in range(1, GROUPS)] + [((TOTAL, HD), F32)] * 2,
        1000000,
    )
    return lax.all_to_all(merged, "head", split_axis=0, concat_axis=1, tiled=True)


def solution(mesh):
    placed = (P("seq", "head"), P("seq", "head"), P("seq", "head"), P())
    return jax.shard_map(
        on_device, mesh=mesh, in_specs=placed, out_specs=P(("seq", "head"), None), check_vma=False
    )
```

```python
import functools
import math

import jax
import jax.numpy as jnp
from jax import lax
from jax.experimental import pallas as pl
from jax.experimental.pallas import tpu as pltpu
from jax.sharding import PartitionSpec as P

ROWS = 768
HD = 128
CHUNK = 256
LANES = 8
GROUPS = 8
BRANCHES = 4
PICKED = (0, 384, 192, 96)
START = (0, 0, 384, 576)
TOTAL = 672
CROSS = (0, 384, 576, 672)
CROSS_START = (0, 0, 384, 960)
VISITING = 1632
CROSS_STEP = (0, 192, 192, 224)
CUT = (0, 0, 384, 384, 576, 576, 576, 576)
SCALE = math.log2(math.e) / math.sqrt(HD)
NEG = -1e30
LOW, HIGH = 2.0**-60, 2.0**120
F32, BF16 = jnp.float32, jnp.bfloat16


def message_rows(d):
    rows = TOTAL - CUT[d]
    sums = -(-rows // 128)
    return rows, sums, rows + -(-3 * sums // 16) * 16


def iota(shape, axis):
    return lax.broadcasted_iota(jnp.int32, shape, axis)


def dot_t(a, b):
    return lax.dot_general(a, b, (((1,), (1,)), ((), ())), preferred_element_type=F32)


def pick_matrix(sm):
    parts = []
    for b in range(1, BRANCHES):
        count, dilation = CHUNK >> b, 1 << b
        hit = iota((count, CHUNK), 1) == iota((count, CHUNK), 0) * dilation + sm[1 + b]
        parts.append(jnp.where(hit, 1.0, 0.0).astype(BF16))
    return jnp.concatenate(parts, axis=0)


def with_ones(values):
    return jnp.concatenate([values, jnp.ones_like(values)], axis=1)


def split3(x):
    high = x.astype(BF16)
    rest = x - high.astype(F32)
    mid = rest.astype(BF16)
    return high, mid, (rest - mid.astype(F32)).astype(BF16)


def pack_kernel(sm, q, k, v, near, kv, q_here, sems):
    copies = [
        pltpu.make_async_copy(q, q_here, sems.at[0]),
        pltpu.make_async_copy(k, kv.at[:, pl.ds(0, HD)], sems.at[1]),
        pltpu.make_async_copy(v, kv.at[:, pl.ds(HD, HD)], sems.at[2]),
    ]
    for copy in copies:
        copy.start()
    pick = pick_matrix(sm)
    copies[0].wait()
    for c in range(ROWS // CHUNK):
        got = jnp.dot(pick, q_here[c * CHUNK : (c + 1) * CHUNK, :], preferred_element_type=F32).astype(BF16)
        for b in range(1, BRANCHES):
            count = CHUNK >> b
            at = CHUNK - (CHUNK >> (b - 1))
            row = START[b] + c * count
            near[row : row + count, :] = got[at : at + count, :]
    copies[1].wait()
    copies[2].wait()


def fast_tile(q, kv, allowed=None):
    total = None
    step = CHUNK if allowed is None and kv.shape[0] % CHUNK == 0 else kv.shape[0]
    for at in range(0, kv.shape[0], step):
        part = kv[at : at + step, :]
        p = jnp.exp2(dot_t(q, part[:, :HD]) * SCALE)
        if allowed is not None:
            p = jnp.where(allowed, p, 0.0)
        added = jnp.dot(p.astype(BF16), with_ones(part[:, HD:]), preferred_element_type=F32)
        total = added if total is None else total + added
    return total


def slow_tile(q, kv, allowed, acc, top, rows):
    s = dot_t(q, kv[:, :HD]) * SCALE
    if allowed is not None:
        s = jnp.where(allowed, s, NEG)
    old = top[rows, :]
    new = jnp.maximum(old, jnp.broadcast_to(jnp.max(s, axis=1, keepdims=True), old.shape))
    factor = jnp.exp2(old - new)
    p = jnp.exp2(s - new[:, :1])
    if allowed is not None:
        p = jnp.where(allowed, p, 0.0)
    added = jnp.dot(p.astype(BF16), with_ones(kv[:, HD:]), preferred_element_type=F32)
    acc[rows, :] = acc[rows, :] * jnp.concatenate([factor, factor], axis=1) + added
    top[rows, :] = new


def in_range(total):
    return (jnp.min(total) >= LOW) & (jnp.max(total) <= HIGH)


def select_keys(sm, pair, keys, part):
    pick = pick_matrix(sm)
    for c in range(2 * ROWS // CHUNK):
        got = jnp.dot(pick, pair[c * CHUNK : (c + 1) * CHUNK, :], preferred_element_type=F32).astype(BF16)
        for b in range(1, BRANCHES):
            count = CHUNK >> b
            at = CHUNK - (CHUNK >> (b - 1))
            row = part * 2 * PICKED[b] + c * count
            keys[b][row : row + count, :] = got[at : at + count, :]


def add_cross(q, keys, acc, parts, first):
    for b in range(1, BRANCHES):
        size = 2 * PICKED[b]
        step = CROSS_STEP[b]
        for at in range(0, CROSS[b], step):
            rows = pl.ds(CROSS_START[b] + at, step)
            total = None if first else acc[rows, :]
            for part in parts:
                added = fast_tile(q[rows, :], keys[b][part * size : (part + 1) * size, :])
                total = added if total is None else total + added
            acc[rows, :] = total


def add_own(q, own_q, pair, keys, part, acc):
    for c in range(ROWS // CHUNK):
        rows = pl.ds(c * CHUNK, CHUNK)
        acc[rows, :] += fast_tile(q[rows, :], pair[:ROWS, :]) + fast_tile(q[rows, :], pair[ROWS:, :])
    for b in range(1, BRANCHES):
        size = 2 * PICKED[b]
        step = min(192, PICKED[b])
        for at in range(0, PICKED[b], step):
            start = START[b] + at
            rows = pl.ds(ROWS + start, step)
            acc[rows, :] += fast_tile(own_q[start : start + step, :], keys[b][part * size : (part + 1) * size, :])


def early_kernel(sm, pair0, pair1, pair2, q, near, r1, r2, r4, r6, visiting, cross, own, *keys):
    keys = (None,) + keys
    core = lax.rem(sm[1], 2)
    visiting[0:384, :] = r1[0:384, :]
    visiting[384:576, :] = r1[384:576, :]
    visiting[576:768, :] = r2[0:192, :]
    visiting[768:960, :] = r2[288:480, :]
    visiting[960:1056, :] = r1[576:672, :]
    visiting[1056:1152, :] = r2[192:288, :]
    visiting[1152:1248, :] = r2[480:576, :]
    visiting[1248:1440, :] = r4[...]
    visiting[1440:1632, :] = r6[...]
    for part, pair in enumerate((pair0, pair1, pair2)):
        select_keys(sm, pair, keys, part)
    add_cross(visiting, keys, cross, (0, 1, 2), True)
    lower = iota((CHUNK, CHUNK), 1) <= iota((CHUNK, CHUNK), 0)
    for c in range(ROWS // CHUNK):
        rows = pl.ds(c * CHUNK, CHUNK)
        start = pl.multiple_of(core * ROWS, ROWS)
        total = fast_tile(q[rows, :], pair0[pl.ds(start + c * CHUNK, CHUNK), :], lower)
        if c:
            total = total + fast_tile(q[rows, :], pair0[pl.ds(start, c * CHUNK), :])
        own[rows, :] = total
    for b in range(1, BRANCHES):
        size = PICKED[b]
        lower = iota((size, size), 1) <= iota((size, size), 0)
        own[ROWS + START[b] : ROWS + START[b] + size, :] = fast_tile(
            near[START[b] : START[b] + size, :], keys[b][pl.ds(pl.multiple_of(core * size, size), size), :], lower
        )

    @pl.when(core == 1)
    def _():
        for c in range(ROWS // CHUNK):
            rows = pl.ds(c * CHUNK, CHUNK)
            own[rows, :] += fast_tile(q[rows, :], pair0[:ROWS, :])
        for b in range(1, BRANCHES):
            size = PICKED[b]
            rows = pl.ds(ROWS + START[b], size)
            own[rows, :] += fast_tile(near[START[b] : START[b] + size, :], keys[b][:size, :])

    @pl.when(before(sm, 1))
    def _():
        add_own(q, near, pair1, keys, 1, own)


def before(sm, stage):
    z = sm[1] // 2
    return jnp.bitwise_xor(z, stage) < z


def last_cross_kernel(sm, *refs):
    pairs, refs = refs[:4], refs[4:]
    visiting, cross, refs = refs[0], refs[2], refs[3:]
    outs, refs = (None,) + refs[:7], refs[7:]
    keys, top, sums = (None,) + refs[:3], refs[3], (None,) + refs[4:11]
    select_keys(sm, pairs[3], keys, 0)
    add_cross(visiting, keys, cross, (0,), False)
    top[...] = jnp.zeros_like(top)

    @pl.when(jnp.logical_not(in_range(cross[:, HD:])))
    def _():
        cross[...] = jnp.zeros_like(cross)
        top[...] = jnp.full_like(top, NEG)
        for pair in pairs:
            select_keys(sm, pair, keys, 0)
            for b in range(1, BRANCHES):

                def step(i, carry, b=b):
                    rows = pl.ds(pl.multiple_of(CROSS_START[b] + i * 96, 96), 96)
                    slow_tile(visiting[rows, :], keys[b], None, cross, top, rows)
                    return carry

                lax.fori_loop(0, CROSS[b] // 96, step, 0)

    for d in range(1, GROUPS):
        sums[d][...] = jnp.zeros_like(sums[d])
    for b in range(1, BRANCHES):
        for d in range(1, 1 << b):
            row = CROSS_START[b] + (d - 1) * PICKED[b]
            rows = slice(row, row + PICKED[b])
            total = cross[rows, HD:]
            at = START[b] - CUT[d]
            outs[d][at : at + PICKED[b], :] = (cross[rows, :HD] / total).astype(BF16)
            sums[d][at : at + PICKED[b], :] = top[rows, :] + jnp.log2(total)
    diagonal = iota((128, 128), 0) == iota((128, 128), 1)
    for d in range(1, GROUPS):
        rows, count, padded = message_rows(d)
        tail = jnp.zeros((padded - rows, 128), F32)
        place = iota(tail.shape, 0)
        for c in range(count):
            line = jnp.sum(jnp.where(diagonal, sums[d][c * 128 : (c + 1) * 128, :], 0.0), axis=0, keepdims=True)
            for n, piece in enumerate(split3(line)):
                tail = jnp.where(place == 3 * c + n, jnp.broadcast_to(piece.astype(F32), tail.shape), tail)
        outs[d][rows:padded, :] = tail.astype(BF16)


def last_own_kernel(sm, *refs):
    pairs, refs = refs[:4], refs[4:]
    q, near, own, out, log_sum, refs = refs[0], refs[1], refs[3], refs[4], refs[5], refs[6:]
    keys, top = (None,) + refs[:3], refs[3]
    lane = sm[1]

    for part in (2, 3):

        @pl.when(before(sm, part))
        def _(part=part):
            select_keys(sm, pairs[part], keys, 0)
            add_own(q, near, pairs[part], keys, 0, own)

    top[...] = jnp.zeros_like(top)

    @pl.when(jnp.logical_not(in_range(own[:, HD:])))
    def _():
        own[...] = jnp.zeros_like(own)
        top[...] = jnp.full_like(top, NEG)
        for n, pair in enumerate(pairs):
            select_keys(sm, pair, keys, 0)
            for core in range(2):
                block = 2 * jnp.bitwise_xor(lane // 2, n) + core

                @pl.when(block <= lane)
                def _(pair=pair, core=core, block=block):
                    for b in range(BRANCHES):
                        size = ROWS >> b
                        source, key = (q, pair) if b == 0 else (near, keys[b])

                        def step(i, carry, b=b, size=size, source=source, key=key):
                            at = pl.multiple_of(START[b] + i * 96, 96)
                            rows = pl.ds(pl.multiple_of((ROWS if b else 0) + at, 96), 96)
                            row = iota((96, size), 0) + i * 96 + lane * size
                            col = iota((96, size), 1) + block * size
                            part = key[core * size : (core + 1) * size, :]
                            slow_tile(source[pl.ds(at, 96), :], part, col <= row, own, top, rows)
                            return carry

                        lax.fori_loop(0, size // 96, step, 0)

    total = own[:, HD:]
    out[...] = own[:, :HD] / total
    log_sum[...] = top[...] + jnp.log2(total)


def merge_kernel(sm, *refs):
    got, refs = (None,) + refs[:7], refs[7:]
    own_out, own_sum, merged, got_sums = refs[0], refs[1], refs[2], (None,) + refs[3:10]
    compact, compact_sum = refs[10], refs[11]
    group = sm[0]
    diagonal = iota((128, 128), 0) == iota((128, 128), 1)
    ones = jnp.ones((128, 128), BF16)
    for d in range(1, GROUPS):
        rows, count, _ = message_rows(d)
        for c in range(count):
            total = jnp.zeros((128, 128), F32)
            for n in range(3):
                line = got[d][rows + 3 * c + n : rows + 3 * c + n + 1, :]
                spread = jnp.where(diagonal, jnp.broadcast_to(line.astype(F32), (128, 128)), 0.0).astype(BF16)
                total = total + jnp.dot(spread, ones, preferred_element_type=F32)
            got_sums[d][c * 128 : (c + 1) * 128, :] = total
    for b in range(1, BRANCHES):
        own, first = PICKED[b], START[b]
        outs = [own_out[ROWS + first : ROWS + first + own, :]]
        logs = [own_sum[ROWS + first : ROWS + first + own, :]]
        for d in range(1, 1 << b):
            at = first - CUT[d]
            valid = jnp.bitwise_xor(group, d) < group
            outs.append(got[d][at : at + own, :].astype(F32))
            logs.append(jnp.where(valid, got_sums[d][at : at + own, :], NEG))
        best = logs[0]
        for log in logs[1:]:
            best = jnp.maximum(best, log)
        top = jnp.zeros_like(best)
        bottom = jnp.zeros_like(best)
        for out, log in zip(outs, logs):
            weight = jnp.exp2(log - best)
            top = top + weight * out
            bottom = bottom + weight
        compact[first : first + own, :] = top / bottom
        compact_sum[first : first + own, :] = best + jnp.log2(bottom)
    for c in range(ROWS // CHUNK):
        rows = slice(c * CHUNK, (c + 1) * CHUNK)
        outs = [own_out[rows, :]]
        logs = [own_sum[rows, :]]
        for b in range(1, BRANCHES):
            count, dilation = CHUNK >> b, 1 << b
            at = START[b] + c * count
            offset = sm[1 + b]
            place = jnp.where(
                iota((CHUNK, count), 0) == iota((CHUNK, count), 1) * dilation + offset, 1.0, 0.0
            ).astype(BF16)
            out_parts = split3(compact[at : at + count, :])
            log_parts = split3(compact_sum[at : at + count, :])
            first = jnp.concatenate([out_parts[0], log_parts[0]], axis=1)
            second = jnp.concatenate([out_parts[1], log_parts[1]], axis=1)
            spread = jnp.dot(place, first, preferred_element_type=F32)
            spread = spread + jnp.dot(place, second, preferred_element_type=F32)
            log = spread[:, HD:] + jnp.dot(place, log_parts[2], preferred_element_type=F32)
            chosen = lax.rem(iota((CHUNK, HD), 0), dilation) == offset
            outs.append(spread[:, :HD])
            logs.append(jnp.where(chosen, log, NEG))
        best = logs[0]
        for log in logs[1:]:
            best = jnp.maximum(best, log)
        top = jnp.zeros_like(best)
        bottom = jnp.zeros_like(best)
        for out, log in zip(outs, logs):
            weight = jnp.exp2(log - best)
            top = top + weight * out
            bottom = bottom + weight
        merged[rows, :] = (top / bottom).astype(BF16)


def call(kernel, name, sm, operands, outputs, scratch, flops, aliases=None):
    shapes = [jax.ShapeDtypeStruct(shape, dtype) for shape, dtype in outputs]
    moved = sum(math.prod(x.shape) * x.dtype.itemsize for x in list(operands) + shapes)
    return pl.pallas_call(
        kernel,
        name=name,
        out_shape=shapes,
        in_specs=[pl.BlockSpec(memory_space=pltpu.SMEM)]
        + [pl.BlockSpec(memory_space=pltpu.VMEM)] * len(operands),
        out_specs=[pl.BlockSpec(memory_space=pltpu.VMEM)] * len(shapes),
        scratch_shapes=[pltpu.VMEM(shape, dtype) for shape, dtype in scratch],
        input_output_aliases=aliases or {},
        compiler_params=pltpu.CompilerParams(vmem_limit_bytes=32 * 1024 * 1024),
        cost_estimate=pl.CostEstimate(flops=1, bytes_accessed=1, transcendentals=0),
    )(sm, *operands)


def pack(sm, q, k, v):
    return pl.pallas_call(
        pack_kernel,
        name="pack",
        out_shape=[jax.ShapeDtypeStruct((TOTAL, HD), BF16), jax.ShapeDtypeStruct((ROWS, 2 * HD), BF16)],
        in_specs=[pl.BlockSpec(memory_space=pltpu.SMEM)] + [pl.BlockSpec(memory_space=pl.ANY)] * 3,
        out_specs=[pl.BlockSpec(memory_space=pltpu.VMEM)] * 2,
        scratch_shapes=[pltpu.VMEM((ROWS, HD), BF16), pltpu.SemaphoreType.DMA((3,))],
        cost_estimate=pl.CostEstimate(flops=1, bytes_accessed=1, transcendentals=0),
    )(sm, q, k, v)


def place_of(index):
    x, z, core = index // 16, index // 2 % 8, index % 2
    return 2 * x + z // 4, z % 4, core


def index_of(group, z, core):
    return (group // 2 * 8 + group % 2 * 4 + z) * 2 + core


def partner(index, j):
    group, z, core = place_of(index)
    return index_of(group ^ j, z ^ 2 if j % 2 else z, core)


def meet(j):
    return [(index, partner(index, j)) for index in range(64)]


def to_later(j):
    return [(index, other) for index, other in meet(j) if place_of(other)[0] > place_of(index)[0]]


def exchange(step):
    pairs = []
    for index in range(64):
        group, z, core = place_of(index)
        pairs.append((index, index_of(group, z ^ step, core)))
    return pairs


def both_cores(block):
    groups = [[i, i + 1] for i in range(0, 64, 2)]
    return lax.all_gather(block, "seq", axis_index_groups=groups, tiled=True)


def on_device(queries, key_rows, values, offsets):
    seq, head = lax.axis_index("seq"), lax.axis_index("head")
    mine = lax.dynamic_slice_in_dim(offsets, head, 1, axis=1)[:, 0]
    sm = jnp.concatenate([jnp.stack([seq // 8, seq % 8]).astype(jnp.int32), mine[1:], jnp.zeros((3,), jnp.int32)])
    near, kv = pack(sm, queries, key_rows, values)
    keys = [((ROWS, 2 * HD), BF16), ((384, 2 * HD), BF16), ((192, 2 * HD), BF16)]
    state = [((VISITING, 2 * HD), F32), ((ROWS + TOTAL, 2 * HD), F32)]
    work = 4 * HD * 2 * ROWS * 2 * ROWS
    r1 = lax.ppermute(near, "seq", meet(1))
    block2 = lax.ppermute(kv, "seq", exchange(2))
    block1 = lax.ppermute(kv, "seq", exchange(1))
    r2 = lax.ppermute(jnp.concatenate([near[384:], r1[384:]]), "seq", meet(2))
    pair3 = jnp.concatenate([near[576:], r1[576:]])
    r4 = lax.ppermute(pair3, "seq", meet(4))
    r6 = lax.ppermute(pair3, "seq", meet(6))
    pairs = [both_cores(kv), both_cores(block1)]
    block2, r2, r4, r6, pairs[1] = lax.optimization_barrier((block2, r2, r4, r6, pairs[1]))
    block3 = lax.ppermute(block2, "seq", exchange(1))
    pairs.append(both_cores(block2))
    visiting, cross, own = call(
        early_kernel,
        "three_chips",
        sm,
        pairs + [queries, near, r1, r2, r4, r6],
        [((VISITING, HD), BF16)] + state,
        [((3 * rows, width), dtype) for (rows, width), dtype in keys],
        work,
    )
    block3, own = lax.optimization_barrier((block3, own))
    pairs.append(both_cores(block3))
    crossed = call(
        last_cross_kernel,
        "cross_end",
        sm,
        pairs + [visiting, cross],
        state[:1] + [((message_rows(d)[2], HD), BF16) for d in range(1, GROUPS)],
        keys + [((VISITING, HD), F32)] + [((message_rows(d)[1] * 128, 128), F32) for d in range(1, GROUPS)],
        work // 2,
        {6: 0},
    )
    back = [lax.ppermute(crossed[j], "seq", to_later(j)) for j in range(1, 6)]
    for j in (6, 7):
        message, back[j - 6] = lax.optimization_barrier((crossed[j], back[j - 6]))
        back.append(lax.ppermute(message, "seq", to_later(j)))
    _, out, log_sum = call(
        last_own_kernel,
        "own_end",
        sm,
        pairs + [queries, near, own],
        state[1:] + [((ROWS + TOTAL, HD), F32)] * 2,
        keys + [((ROWS + TOTAL, HD), F32)],
        work // 2,
        {7: 0},
    )
    (merged,) = call(
        merge_kernel,
        "merge",
        sm,
        back + [out, log_sum],
        [((ROWS, HD), BF16)],
        [((message_rows(d)[1] * 128, 128), F32) for d in range(1, GROUPS)] + [((TOTAL, HD), F32)] * 2,
        1000000,
    )
    return lax.all_to_all(merged, "head", split_axis=0, concat_axis=1, tiled=True)


def solution(mesh):
    placed = (P("seq", "head"), P("seq", "head"), P("seq", "head"), P())
    return jax.shard_map(
        on_device, mesh=mesh, in_specs=placed, out_specs=P(("seq", "head"), None), check_vma=False
    )
```

```python
import functools
import math

import jax
import jax.numpy as jnp
from jax import lax
from jax.experimental import pallas as pl
from jax.experimental.pallas import tpu as pltpu
from jax.sharding import PartitionSpec as P

ROWS = 768
HD = 128
CHUNK = 256
LANES = 8
GROUPS = 8
BRANCHES = 4
PICKED = (0, 384, 192, 96)
START = (0, 0, 384, 576)
TOTAL = 672
CROSS = (0, 384, 576, 672)
CROSS_START = (0, 0, 384, 960)
VISITING = 1632
CROSS_STEP = (0, 192, 192, 224)
CUT = (0, 0, 384, 384, 576, 576, 576, 576)
SCALE = math.log2(math.e) / math.sqrt(HD)
NEG = -1e30
LOW, HIGH = 2.0**-60, 2.0**120
F32, BF16 = jnp.float32, jnp.bfloat16


def message_rows(d):
    rows = TOTAL - CUT[d]
    sums = -(-rows // 128)
    return rows, sums, rows + -(-3 * sums // 16) * 16


def iota(shape, axis):
    return lax.broadcasted_iota(jnp.int32, shape, axis)


def dot_t(a, b):
    return lax.dot_general(a, b, (((1,), (1,)), ((), ())), preferred_element_type=F32)


def pick_matrix(sm):
    parts = []
    for b in range(1, BRANCHES):
        count, dilation = CHUNK >> b, 1 << b
        hit = iota((count, CHUNK), 1) == iota((count, CHUNK), 0) * dilation + sm[1 + b]
        parts.append(jnp.where(hit, 1.0, 0.0).astype(BF16))
    return jnp.concatenate(parts, axis=0)


def with_ones(values):
    return jnp.concatenate([values, jnp.ones_like(values)], axis=1)


def split3(x):
    high = x.astype(BF16)
    rest = x - high.astype(F32)
    mid = rest.astype(BF16)
    return high, mid, (rest - mid.astype(F32)).astype(BF16)


def pack_kernel(sm, q, k, v, near, kv, q_here, sems):
    copies = [
        pltpu.make_async_copy(q, q_here, sems.at[0]),
        pltpu.make_async_copy(k, kv.at[:, pl.ds(0, HD)], sems.at[1]),
        pltpu.make_async_copy(v, kv.at[:, pl.ds(HD, HD)], sems.at[2]),
    ]
    for copy in copies:
        copy.start()
    pick = pick_matrix(sm)
    copies[0].wait()
    for c in range(ROWS // CHUNK):
        got = jnp.dot(pick, q_here[c * CHUNK : (c + 1) * CHUNK, :], preferred_element_type=F32).astype(BF16)
        for b in range(1, BRANCHES):
            count = CHUNK >> b
            at = CHUNK - (CHUNK >> (b - 1))
            row = START[b] + c * count
            near[row : row + count, :] = got[at : at + count, :]
    copies[1].wait()
    copies[2].wait()


def fast_tile(q, kv, allowed=None):
    total = None
    step = CHUNK if allowed is None and kv.shape[0] % CHUNK == 0 else kv.shape[0]
    for at in range(0, kv.shape[0], step):
        part = kv[at : at + step, :]
        p = jnp.exp2(dot_t(q, part[:, :HD]) * SCALE)
        if allowed is not None:
            p = jnp.where(allowed, p, 0.0)
        added = jnp.dot(p.astype(BF16), with_ones(part[:, HD:]), preferred_element_type=F32)
        total = added if total is None else total + added
    return total


def slow_tile(q, kv, allowed, acc, top, rows):
    s = dot_t(q, kv[:, :HD]) * SCALE
    if allowed is not None:
        s = jnp.where(allowed, s, NEG)
    old = top[rows, :]
    new = jnp.maximum(old, jnp.broadcast_to(jnp.max(s, axis=1, keepdims=True), old.shape))
    factor = jnp.exp2(old - new)
    p = jnp.exp2(s - new[:, :1])
    if allowed is not None:
        p = jnp.where(allowed, p, 0.0)
    added = jnp.dot(p.astype(BF16), with_ones(kv[:, HD:]), preferred_element_type=F32)
    acc[rows, :] = acc[rows, :] * jnp.concatenate([factor, factor], axis=1) + added
    top[rows, :] = new


def in_range(total):
    return (jnp.min(total) >= LOW) & (jnp.max(total) <= HIGH)


def select_keys(sm, pair, keys, part):
    pick = pick_matrix(sm)
    for c in range(2 * ROWS // CHUNK):
        got = jnp.dot(pick, pair[c * CHUNK : (c + 1) * CHUNK, :], preferred_element_type=F32).astype(BF16)
        for b in range(1, BRANCHES):
            count = CHUNK >> b
            at = CHUNK - (CHUNK >> (b - 1))
            row = part * 2 * PICKED[b] + c * count
            keys[b][row : row + count, :] = got[at : at + count, :]


def add_cross(q, keys, acc, parts, first):
    for b in range(1, BRANCHES):
        size = 2 * PICKED[b]
        step = CROSS_STEP[b]
        for at in range(0, CROSS[b], step):
            rows = pl.ds(CROSS_START[b] + at, step)
            total = None if first else acc[rows, :]
            for part in parts:
                added = fast_tile(q[rows, :], keys[b][part * size : (part + 1) * size, :])
                total = added if total is None else total + added
            acc[rows, :] = total


def add_own(q, own_q, pair, keys, part, acc):
    for c in range(ROWS // CHUNK):
        rows = pl.ds(c * CHUNK, CHUNK)
        acc[rows, :] += fast_tile(q[rows, :], pair[:ROWS, :]) + fast_tile(q[rows, :], pair[ROWS:, :])
    for b in range(1, BRANCHES):
        size = 2 * PICKED[b]
        step = min(192, PICKED[b])
        for at in range(0, PICKED[b], step):
            start = START[b] + at
            rows = pl.ds(ROWS + start, step)
            acc[rows, :] += fast_tile(own_q[start : start + step, :], keys[b][part * size : (part + 1) * size, :])


def early_kernel(sm, pair0, pair1, pair2, q, near, r1, r2, r4, visiting, cross, own, *keys):
    keys = (None,) + keys
    core = lax.rem(sm[1], 2)
    visiting[0:384, :] = r1[0:384, :]
    visiting[384:576, :] = r1[384:576, :]
    visiting[576:768, :] = r2[0:192, :]
    visiting[768:960, :] = r2[288:480, :]
    visiting[960:1056, :] = r1[576:672, :]
    visiting[1056:1152, :] = r2[192:288, :]
    visiting[1152:1248, :] = r2[480:576, :]
    visiting[1248:1632, :] = r4[...]
    for part, pair in enumerate((pair0, pair1, pair2)):
        select_keys(sm, pair, keys, part)
    add_cross(visiting, keys, cross, (0, 1, 2), True)
    lower = iota((CHUNK, CHUNK), 1) <= iota((CHUNK, CHUNK), 0)
    for c in range(ROWS // CHUNK):
        rows = pl.ds(c * CHUNK, CHUNK)
        start = pl.multiple_of(core * ROWS, ROWS)
        total = fast_tile(q[rows, :], pair0[pl.ds(start + c * CHUNK, CHUNK), :], lower)
        if c:
            total = total + fast_tile(q[rows, :], pair0[pl.ds(start, c * CHUNK), :])
        own[rows, :] = total
    for b in range(1, BRANCHES):
        size = PICKED[b]
        lower = iota((size, size), 1) <= iota((size, size), 0)
        own[ROWS + START[b] : ROWS + START[b] + size, :] = fast_tile(
            near[START[b] : START[b] + size, :], keys[b][pl.ds(pl.multiple_of(core * size, size), size), :], lower
        )

    @pl.when(core == 1)
    def _():
        for c in range(ROWS // CHUNK):
            rows = pl.ds(c * CHUNK, CHUNK)
            own[rows, :] += fast_tile(q[rows, :], pair0[:ROWS, :])
        for b in range(1, BRANCHES):
            size = PICKED[b]
            rows = pl.ds(ROWS + START[b], size)
            own[rows, :] += fast_tile(near[START[b] : START[b] + size, :], keys[b][:size, :])

    @pl.when(before(sm, 1))
    def _():
        add_own(q, near, pair1, keys, 1, own)


def before(sm, stage):
    z = sm[1] // 2
    return jnp.bitwise_xor(z, stage) < z


def last_cross_kernel(sm, *refs):
    pairs, refs = refs[:4], refs[4:]
    visiting, cross, refs = refs[0], refs[2], refs[3:]
    outs, refs = (None,) + refs[:7], refs[7:]
    keys, top, sums = (None,) + refs[:3], refs[3], (None,) + refs[4:11]
    select_keys(sm, pairs[3], keys, 0)
    add_cross(visiting, keys, cross, (0,), False)
    top[...] = jnp.zeros_like(top)

    @pl.when(jnp.logical_not(in_range(cross[:, HD:])))
    def _():
        cross[...] = jnp.zeros_like(cross)
        top[...] = jnp.full_like(top, NEG)
        for pair in pairs:
            select_keys(sm, pair, keys, 0)
            for b in range(1, BRANCHES):

                def step(i, carry, b=b):
                    rows = pl.ds(pl.multiple_of(CROSS_START[b] + i * 96, 96), 96)
                    slow_tile(visiting[rows, :], keys[b], None, cross, top, rows)
                    return carry

                lax.fori_loop(0, CROSS[b] // 96, step, 0)

    for d in range(1, GROUPS):
        sums[d][...] = jnp.zeros_like(sums[d])
    for b in range(1, BRANCHES):
        for d in range(1, 1 << b):
            row = CROSS_START[b] + (d - 1) * PICKED[b]
            rows = slice(row, row + PICKED[b])
            total = cross[rows, HD:]
            at = START[b] - CUT[d]
            outs[d][at : at + PICKED[b], :] = (cross[rows, :HD] / total).astype(BF16)
            sums[d][at : at + PICKED[b], :] = top[rows, :] + jnp.log2(total)
    diagonal = iota((128, 128), 0) == iota((128, 128), 1)
    for d in range(1, GROUPS):
        rows, count, padded = message_rows(d)
        tail = jnp.zeros((padded - rows, 128), F32)
        place = iota(tail.shape, 0)
        for c in range(count):
            line = jnp.sum(jnp.where(diagonal, sums[d][c * 128 : (c + 1) * 128, :], 0.0), axis=0, keepdims=True)
            for n, piece in enumerate(split3(line)):
                tail = jnp.where(place == 3 * c + n, jnp.broadcast_to(piece.astype(F32), tail.shape), tail)
        outs[d][rows:padded, :] = tail.astype(BF16)


def last_own_kernel(sm, *refs):
    pairs, refs = refs[:4], refs[4:]
    q, near, own, out, log_sum, refs = refs[0], refs[1], refs[3], refs[4], refs[5], refs[6:]
    keys, top = (None,) + refs[:3], refs[3]
    lane = sm[1]

    for part in (2, 3):

        @pl.when(before(sm, part))
        def _(part=part):
            select_keys(sm, pairs[part], keys, 0)
            add_own(q, near, pairs[part], keys, 0, own)

    top[...] = jnp.zeros_like(top)

    @pl.when(jnp.logical_not(in_range(own[:, HD:])))
    def _():
        own[...] = jnp.zeros_like(own)
        top[...] = jnp.full_like(top, NEG)
        for n, pair in enumerate(pairs):
            select_keys(sm, pair, keys, 0)
            for core in range(2):
                block = 2 * jnp.bitwise_xor(lane // 2, n) + core

                @pl.when(block <= lane)
                def _(pair=pair, core=core, block=block):
                    for b in range(BRANCHES):
                        size = ROWS >> b
                        source, key = (q, pair) if b == 0 else (near, keys[b])

                        def step(i, carry, b=b, size=size, source=source, key=key):
                            at = pl.multiple_of(START[b] + i * 96, 96)
                            rows = pl.ds(pl.multiple_of((ROWS if b else 0) + at, 96), 96)
                            row = iota((96, size), 0) + i * 96 + lane * size
                            col = iota((96, size), 1) + block * size
                            part = key[core * size : (core + 1) * size, :]
                            slow_tile(source[pl.ds(at, 96), :], part, col <= row, own, top, rows)
                            return carry

                        lax.fori_loop(0, size // 96, step, 0)

    total = own[:, HD:]
    out[...] = own[:, :HD] / total
    log_sum[...] = top[...] + jnp.log2(total)


def merge_kernel(sm, *refs):
    got, refs = (None,) + refs[:7], refs[7:]
    own_out, own_sum, merged, got_sums = refs[0], refs[1], refs[2], (None,) + refs[3:10]
    compact, compact_sum = refs[10], refs[11]
    group = sm[0]
    diagonal = iota((128, 128), 0) == iota((128, 128), 1)
    ones = jnp.ones((128, 128), BF16)
    for d in range(1, GROUPS):
        rows, count, _ = message_rows(d)
        for c in range(count):
            total = jnp.zeros((128, 128), F32)
            for n in range(3):
                line = got[d][rows + 3 * c + n : rows + 3 * c + n + 1, :]
                spread = jnp.where(diagonal, jnp.broadcast_to(line.astype(F32), (128, 128)), 0.0).astype(BF16)
                total = total + jnp.dot(spread, ones, preferred_element_type=F32)
            got_sums[d][c * 128 : (c + 1) * 128, :] = total
    for b in range(1, BRANCHES):
        own, first = PICKED[b], START[b]
        outs = [own_out[ROWS + first : ROWS + first + own, :]]
        logs = [own_sum[ROWS + first : ROWS + first + own, :]]
        for d in range(1, 1 << b):
            at = first - CUT[d]
            valid = jnp.bitwise_xor(group, d) < group
            outs.append(got[d][at : at + own, :].astype(F32))
            logs.append(jnp.where(valid, got_sums[d][at : at + own, :], NEG))
        best = logs[0]
        for log in logs[1:]:
            best = jnp.maximum(best, log)
        top = jnp.zeros_like(best)
        bottom = jnp.zeros_like(best)
        for out, log in zip(outs, logs):
            weight = jnp.exp2(log - best)
            top = top + weight * out
            bottom = bottom + weight
        compact[first : first + own, :] = top / bottom
        compact_sum[first : first + own, :] = best + jnp.log2(bottom)
    for c in range(ROWS // CHUNK):
        rows = slice(c * CHUNK, (c + 1) * CHUNK)
        outs = [own_out[rows, :]]
        logs = [own_sum[rows, :]]
        for b in range(1, BRANCHES):
            count, dilation = CHUNK >> b, 1 << b
            at = START[b] + c * count
            offset = sm[1 + b]
            place = jnp.where(
                iota((CHUNK, count), 0) == iota((CHUNK, count), 1) * dilation + offset, 1.0, 0.0
            ).astype(BF16)
            out_parts = split3(compact[at : at + count, :])
            log_parts = split3(compact_sum[at : at + count, :])
            first = jnp.concatenate([out_parts[0], log_parts[0]], axis=1)
            second = jnp.concatenate([out_parts[1], log_parts[1]], axis=1)
            spread = jnp.dot(place, first, preferred_element_type=F32)
            spread = spread + jnp.dot(place, second, preferred_element_type=F32)
            log = spread[:, HD:] + jnp.dot(place, log_parts[2], preferred_element_type=F32)
            chosen = lax.rem(iota((CHUNK, HD), 0), dilation) == offset
            outs.append(spread[:, :HD])
            logs.append(jnp.where(chosen, log, NEG))
        best = logs[0]
        for log in logs[1:]:
            best = jnp.maximum(best, log)
        top = jnp.zeros_like(best)
        bottom = jnp.zeros_like(best)
        for out, log in zip(outs, logs):
            weight = jnp.exp2(log - best)
            top = top + weight * out
            bottom = bottom + weight
        merged[rows, :] = (top / bottom).astype(BF16)


def call(kernel, name, sm, operands, outputs, scratch, flops, aliases=None):
    shapes = [jax.ShapeDtypeStruct(shape, dtype) for shape, dtype in outputs]
    moved = sum(math.prod(x.shape) * x.dtype.itemsize for x in list(operands) + shapes)
    return pl.pallas_call(
        kernel,
        name=name,
        out_shape=shapes,
        in_specs=[pl.BlockSpec(memory_space=pltpu.SMEM)]
        + [pl.BlockSpec(memory_space=pltpu.VMEM)] * len(operands),
        out_specs=[pl.BlockSpec(memory_space=pltpu.VMEM)] * len(shapes),
        scratch_shapes=[pltpu.VMEM(shape, dtype) for shape, dtype in scratch],
        input_output_aliases=aliases or {},
        compiler_params=pltpu.CompilerParams(vmem_limit_bytes=32 * 1024 * 1024),
        cost_estimate=pl.CostEstimate(flops=1, bytes_accessed=1, transcendentals=0),
    )(sm, *operands)


def pack(sm, q, k, v):
    return pl.pallas_call(
        pack_kernel,
        name="pack",
        out_shape=[jax.ShapeDtypeStruct((TOTAL, HD), BF16), jax.ShapeDtypeStruct((ROWS, 2 * HD), BF16)],
        in_specs=[pl.BlockSpec(memory_space=pltpu.SMEM)] + [pl.BlockSpec(memory_space=pl.ANY)] * 3,
        out_specs=[pl.BlockSpec(memory_space=pltpu.VMEM)] * 2,
        scratch_shapes=[pltpu.VMEM((ROWS, HD), BF16), pltpu.SemaphoreType.DMA((3,))],
        cost_estimate=pl.CostEstimate(flops=1, bytes_accessed=1, transcendentals=0),
    )(sm, q, k, v)


def place_of(index):
    x, z, core = index // 16, index // 2 % 8, index % 2
    return 2 * x + z // 4, z % 4, core


def index_of(group, z, core):
    return (group // 2 * 8 + group % 2 * 4 + z) * 2 + core


def partner(index, j):
    group, z, core = place_of(index)
    return index_of(group ^ j, z ^ 2 if j % 2 else z, core)


def meet(j):
    return [(index, partner(index, j)) for index in range(64)]


def to_later(j):
    return [(index, other) for index, other in meet(j) if place_of(other)[0] > place_of(index)[0]]


def exchange(step):
    pairs = []
    for index in range(64):
        group, z, core = place_of(index)
        pairs.append((index, index_of(group, z ^ step, core)))
    return pairs


def both_cores(block):
    groups = [[i, i + 1] for i in range(0, 64, 2)]
    return lax.all_gather(block, "seq", axis_index_groups=groups, tiled=True)


def on_device(queries, key_rows, values, offsets):
    seq, head = lax.axis_index("seq"), lax.axis_index("head")
    mine = lax.dynamic_slice_in_dim(offsets, head, 1, axis=1)[:, 0]
    sm = jnp.concatenate([jnp.stack([seq // 8, seq % 8]).astype(jnp.int32), mine[1:], jnp.zeros((3,), jnp.int32)])
    near, kv = pack(sm, queries, key_rows, values)
    keys = [((ROWS, 2 * HD), BF16), ((384, 2 * HD), BF16), ((192, 2 * HD), BF16)]
    state = [((VISITING, 2 * HD), F32), ((ROWS + TOTAL, 2 * HD), F32)]
    work = 4 * HD * 2 * ROWS * 2 * ROWS
    r1 = lax.ppermute(near, "seq", meet(1))
    block2 = lax.ppermute(kv, "seq", exchange(2))
    block1 = lax.ppermute(kv, "seq", exchange(1))
    r2 = lax.ppermute(jnp.concatenate([near[384:], r1[384:]]), "seq", meet(2))
    r4 = lax.ppermute(jnp.concatenate([near[576:], r1[576:], r2[192:288], r2[480:]]), "seq", meet(4))
    pairs = [both_cores(kv), both_cores(block1)]
    block2, r2 = lax.optimization_barrier((block2, r2))
    block3 = lax.ppermute(block2, "seq", exchange(1))
    pairs.append(both_cores(block2))
    visiting, cross, own = call(
        early_kernel,
        "three_chips",
        sm,
        pairs + [queries, near, r1, r2, r4],
        [((VISITING, HD), BF16)] + state,
        [((3 * rows, width), dtype) for (rows, width), dtype in keys],
        work,
    )
    block3, own = lax.optimization_barrier((block3, own))
    pairs.append(both_cores(block3))
    crossed = call(
        last_cross_kernel,
        "cross_end",
        sm,
        pairs + [visiting, cross],
        state[:1] + [((message_rows(d)[2], HD), BF16) for d in range(1, GROUPS)],
        keys + [((VISITING, HD), F32)] + [((message_rows(d)[1] * 128, 128), F32) for d in range(1, GROUPS)],
        work // 2,
        {6: 0},
    )
    back = [lax.ppermute(crossed[j], "seq", to_later(j)) for j in range(1, 6)]
    for j in (6, 7):
        message, back[j - 6] = lax.optimization_barrier((crossed[j], back[j - 6]))
        back.append(lax.ppermute(message, "seq", to_later(j)))
    _, out, log_sum = call(
        last_own_kernel,
        "own_end",
        sm,
        pairs + [queries, near, own],
        state[1:] + [((ROWS + TOTAL, HD), F32)] * 2,
        keys + [((ROWS + TOTAL, HD), F32)],
        work // 2,
        {7: 0},
    )
    (merged,) = call(
        merge_kernel,
        "merge",
        sm,
        back + [out, log_sum],
        [((ROWS, HD), BF16)],
        [((message_rows(d)[1] * 128, 128), F32) for d in range(1, GROUPS)] + [((TOTAL, HD), F32)] * 2,
        1000000,
    )
    return lax.all_to_all(merged, "head", split_axis=0, concat_axis=1, tiled=True)


def solution(mesh):
    placed = (P("seq", "head"), P("seq", "head"), P("seq", "head"), P())
    return jax.shard_map(
        on_device, mesh=mesh, in_specs=placed, out_specs=P(("seq", "head"), None), check_vma=False
    )
```

```python
import functools
import math

import jax
import jax.numpy as jnp
from jax import lax
from jax.experimental import pallas as pl
from jax.experimental.pallas import tpu as pltpu
from jax.sharding import PartitionSpec as P

ROWS = 768
HD = 128
CHUNK = 256
LANES = 8
GROUPS = 8
BRANCHES = 4
PICKED = (0, 384, 192, 96)
START = (0, 0, 384, 576)
TOTAL = 672
CROSS = (0, 384, 576, 672)
CROSS_START = (0, 0, 384, 960)
VISITING = 1632
CROSS_STEP = (0, 192, 192, 224)
CUT = (0, 0, 384, 384, 576, 576, 576, 576)
SCALE = math.log2(math.e) / math.sqrt(HD)
NEG = -1e30
LOW, HIGH = 2.0**-60, 2.0**120
F32, BF16 = jnp.float32, jnp.bfloat16


def message_rows(d):
    rows = TOTAL - CUT[d]
    sums = -(-rows // 128)
    return rows, sums, rows + -(-3 * sums // 16) * 16


def iota(shape, axis):
    return lax.broadcasted_iota(jnp.int32, shape, axis)


def dot_t(a, b):
    return lax.dot_general(a, b, (((1,), (1,)), ((), ())), preferred_element_type=F32)


def pick_matrix(sm):
    parts = []
    for b in range(1, BRANCHES):
        count, dilation = CHUNK >> b, 1 << b
        hit = iota((count, CHUNK), 1) == iota((count, CHUNK), 0) * dilation + sm[1 + b]
        parts.append(jnp.where(hit, 1.0, 0.0).astype(BF16))
    return jnp.concatenate(parts, axis=0)


def with_ones(values):
    return jnp.concatenate([values, jnp.ones_like(values)], axis=1)


def split3(x):
    high = x.astype(BF16)
    rest = x - high.astype(F32)
    mid = rest.astype(BF16)
    return high, mid, (rest - mid.astype(F32)).astype(BF16)


def pack_kernel(sm, q, k, v, near, kv, q_here, sems):
    copies = [
        pltpu.make_async_copy(q, q_here, sems.at[0]),
        pltpu.make_async_copy(k, kv.at[:, pl.ds(0, HD)], sems.at[1]),
        pltpu.make_async_copy(v, kv.at[:, pl.ds(HD, HD)], sems.at[2]),
    ]
    for copy in copies:
        copy.start()
    pick = pick_matrix(sm)
    copies[0].wait()
    for c in range(ROWS // CHUNK):
        got = jnp.dot(pick, q_here[c * CHUNK : (c + 1) * CHUNK, :], preferred_element_type=F32).astype(BF16)
        for b in range(1, BRANCHES):
            count = CHUNK >> b
            at = CHUNK - (CHUNK >> (b - 1))
            row = START[b] + c * count
            near[row : row + count, :] = got[at : at + count, :]
    copies[1].wait()
    copies[2].wait()


def fast_tile(q, kv, allowed=None):
    total = None
    step = CHUNK if allowed is None and kv.shape[0] % CHUNK == 0 else kv.shape[0]
    for at in range(0, kv.shape[0], step):
        part = kv[at : at + step, :]
        p = jnp.exp2(dot_t(q, part[:, :HD]) * SCALE)
        if allowed is not None:
            p = jnp.where(allowed, p, 0.0)
        added = jnp.dot(p.astype(BF16), with_ones(part[:, HD:]), preferred_element_type=F32)
        total = added if total is None else total + added
    return total


def slow_tile(q, kv, allowed, acc, top, rows):
    s = dot_t(q, kv[:, :HD]) * SCALE
    if allowed is not None:
        s = jnp.where(allowed, s, NEG)
    old = top[rows, :]
    new = jnp.maximum(old, jnp.broadcast_to(jnp.max(s, axis=1, keepdims=True), old.shape))
    factor = jnp.exp2(old - new)
    p = jnp.exp2(s - new[:, :1])
    if allowed is not None:
        p = jnp.where(allowed, p, 0.0)
    added = jnp.dot(p.astype(BF16), with_ones(kv[:, HD:]), preferred_element_type=F32)
    acc[rows, :] = acc[rows, :] * jnp.concatenate([factor, factor], axis=1) + added
    top[rows, :] = new


def in_range(total):
    return (jnp.min(total) >= LOW) & (jnp.max(total) <= HIGH)


def select_keys(sm, pair, keys, part):
    pick = pick_matrix(sm)
    for c in range(2 * ROWS // CHUNK):
        got = jnp.dot(pick, pair[c * CHUNK : (c + 1) * CHUNK, :], preferred_element_type=F32).astype(BF16)
        for b in range(1, BRANCHES):
            count = CHUNK >> b
            at = CHUNK - (CHUNK >> (b - 1))
            row = part * 2 * PICKED[b] + c * count
            keys[b][row : row + count, :] = got[at : at + count, :]


def add_cross(q, keys, acc, parts, first):
    for b in range(1, BRANCHES):
        size = 2 * PICKED[b]
        step = CROSS_STEP[b]
        for at in range(0, CROSS[b], step):
            rows = pl.ds(CROSS_START[b] + at, step)
            total = None if first else acc[rows, :]
            for part in parts:
                added = fast_tile(q[rows, :], keys[b][part * size : (part + 1) * size, :])
                total = added if total is None else total + added
            acc[rows, :] = total


def add_own(q, own_q, pair, keys, part, acc):
    for c in range(ROWS // CHUNK):
        rows = pl.ds(c * CHUNK, CHUNK)
        acc[rows, :] += fast_tile(q[rows, :], pair[:ROWS, :]) + fast_tile(q[rows, :], pair[ROWS:, :])
    for b in range(1, BRANCHES):
        size = 2 * PICKED[b]
        step = min(192, PICKED[b])
        for at in range(0, PICKED[b], step):
            start = START[b] + at
            rows = pl.ds(ROWS + start, step)
            acc[rows, :] += fast_tile(own_q[start : start + step, :], keys[b][part * size : (part + 1) * size, :])


def early_kernel(sm, pair0, pair1, pair2, q, near, r1, r2, r4, visiting, cross, own, *keys):
    keys = (None,) + keys
    core = lax.rem(sm[1], 2)
    visiting[0:384, :] = r1[0:384, :]
    visiting[384:576, :] = r1[384:576, :]
    visiting[576:768, :] = r2[0:192, :]
    visiting[768:960, :] = r2[288:480, :]
    visiting[960:1056, :] = r1[576:672, :]
    visiting[1056:1152, :] = r2[192:288, :]
    visiting[1152:1248, :] = r2[480:576, :]
    visiting[1248:1632, :] = r4[...]
    for part, pair in enumerate((pair0, pair1, pair2)):
        select_keys(sm, pair, keys, part)
    add_cross(visiting, keys, cross, (0, 1, 2), True)
    lower = iota((CHUNK, CHUNK), 1) <= iota((CHUNK, CHUNK), 0)
    for c in range(ROWS // CHUNK):
        rows = pl.ds(c * CHUNK, CHUNK)
        start = pl.multiple_of(core * ROWS, ROWS)
        total = fast_tile(q[rows, :], pair0[pl.ds(start + c * CHUNK, CHUNK), :], lower)
        if c:
            total = total + fast_tile(q[rows, :], pair0[pl.ds(start, c * CHUNK), :])
        own[rows, :] = total
    for b in range(1, BRANCHES):
        size = PICKED[b]
        lower = iota((size, size), 1) <= iota((size, size), 0)
        own[ROWS + START[b] : ROWS + START[b] + size, :] = fast_tile(
            near[START[b] : START[b] + size, :], keys[b][pl.ds(pl.multiple_of(core * size, size), size), :], lower
        )

    @pl.when(core == 1)
    def _():
        for c in range(ROWS // CHUNK):
            rows = pl.ds(c * CHUNK, CHUNK)
            own[rows, :] += fast_tile(q[rows, :], pair0[:ROWS, :])
        for b in range(1, BRANCHES):
            size = PICKED[b]
            rows = pl.ds(ROWS + START[b], size)
            own[rows, :] += fast_tile(near[START[b] : START[b] + size, :], keys[b][:size, :])

    @pl.when(before(sm, 1))
    def _():
        add_own(q, near, pair1, keys, 1, own)


def before(sm, stage):
    z = sm[1] // 2
    return jnp.bitwise_xor(z, stage) < z


def last_cross_kernel(sm, *refs):
    pairs, refs = refs[:4], refs[4:]
    visiting, cross, refs = refs[0], refs[2], refs[3:]
    outs, refs = (None,) + refs[:7], refs[7:]
    keys, top, sums = (None,) + refs[:3], refs[3], (None,) + refs[4:11]
    select_keys(sm, pairs[3], keys, 0)
    add_cross(visiting, keys, cross, (0,), False)
    top[...] = jnp.zeros_like(top)

    @pl.when(jnp.logical_not(in_range(cross[:, HD:])))
    def _():
        cross[...] = jnp.zeros_like(cross)
        top[...] = jnp.full_like(top, NEG)
        for pair in pairs:
            select_keys(sm, pair, keys, 0)
            for b in range(1, BRANCHES):

                def step(i, carry, b=b):
                    rows = pl.ds(pl.multiple_of(CROSS_START[b] + i * 96, 96), 96)
                    slow_tile(visiting[rows, :], keys[b], None, cross, top, rows)
                    return carry

                lax.fori_loop(0, CROSS[b] // 96, step, 0)

    for d in range(1, GROUPS):
        sums[d][...] = jnp.zeros_like(sums[d])
    for b in range(1, BRANCHES):
        for d in range(1, 1 << b):
            row = CROSS_START[b] + (d - 1) * PICKED[b]
            rows = slice(row, row + PICKED[b])
            total = cross[rows, HD:]
            at = START[b] - CUT[d]
            outs[d][at : at + PICKED[b], :] = (cross[rows, :HD] / total).astype(BF16)
            sums[d][at : at + PICKED[b], :] = top[rows, :] + jnp.log2(total)
    diagonal = iota((128, 128), 0) == iota((128, 128), 1)
    for d in range(1, GROUPS):
        rows, count, padded = message_rows(d)
        tail = jnp.zeros((padded - rows, 128), F32)
        place = iota(tail.shape, 0)
        for c in range(count):
            line = jnp.sum(jnp.where(diagonal, sums[d][c * 128 : (c + 1) * 128, :], 0.0), axis=0, keepdims=True)
            for n, piece in enumerate(split3(line)):
                tail = jnp.where(place == 3 * c + n, jnp.broadcast_to(piece.astype(F32), tail.shape), tail)
        outs[d][rows:padded, :] = tail.astype(BF16)


def last_own_kernel(sm, *refs):
    pairs, refs = refs[:4], refs[4:]
    q, near, refs = refs[0], refs[1], refs[3:]
    early, late, refs = (None,) + refs[:3], (None,) + refs[3:6], refs[6:]
    own, out, log_sum, refs = refs[0], refs[1], refs[2], refs[3:]
    keys, top = (None,) + refs[:3], refs[3]
    lane = sm[1]

    for part, chosen, at in ((2, early, 2), (3, late, 0)):

        @pl.when(before(sm, part))
        def _(part=part, chosen=chosen, at=at):
            add_own(q, near, pairs[part], chosen, at, own)

    top[...] = jnp.zeros_like(top)

    @pl.when(jnp.logical_not(in_range(own[:, HD:])))
    def _():
        own[...] = jnp.zeros_like(own)
        top[...] = jnp.full_like(top, NEG)
        for n, pair in enumerate(pairs):
            select_keys(sm, pair, keys, 0)
            for core in range(2):
                block = 2 * jnp.bitwise_xor(lane // 2, n) + core

                @pl.when(block <= lane)
                def _(pair=pair, core=core, block=block):
                    for b in range(BRANCHES):
                        size = ROWS >> b
                        source, key = (q, pair) if b == 0 else (near, keys[b])

                        def step(i, carry, b=b, size=size, source=source, key=key):
                            at = pl.multiple_of(START[b] + i * 96, 96)
                            rows = pl.ds(pl.multiple_of((ROWS if b else 0) + at, 96), 96)
                            row = iota((96, size), 0) + i * 96 + lane * size
                            col = iota((96, size), 1) + block * size
                            part = key[core * size : (core + 1) * size, :]
                            slow_tile(source[pl.ds(at, 96), :], part, col <= row, own, top, rows)
                            return carry

                        lax.fori_loop(0, size // 96, step, 0)

    total = own[:, HD:]
    out[...] = own[:, :HD] / total
    log_sum[...] = top[...] + jnp.log2(total)


def merge_kernel(sm, *refs):
    got, refs = (None,) + refs[:7], refs[7:]
    own_out, own_sum, merged, got_sums = refs[0], refs[1], refs[2], (None,) + refs[3:10]
    compact, compact_sum = refs[10], refs[11]
    group = sm[0]
    diagonal = iota((128, 128), 0) == iota((128, 128), 1)
    ones = jnp.ones((128, 128), BF16)
    for d in range(1, GROUPS):
        rows, count, _ = message_rows(d)
        for c in range(count):
            total = jnp.zeros((128, 128), F32)
            for n in range(3):
                line = got[d][rows + 3 * c + n : rows + 3 * c + n + 1, :]
                spread = jnp.where(diagonal, jnp.broadcast_to(line.astype(F32), (128, 128)), 0.0).astype(BF16)
                total = total + jnp.dot(spread, ones, preferred_element_type=F32)
            got_sums[d][c * 128 : (c + 1) * 128, :] = total
    for b in range(1, BRANCHES):
        own, first = PICKED[b], START[b]
        outs = [own_out[ROWS + first : ROWS + first + own, :]]
        logs = [own_sum[ROWS + first : ROWS + first + own, :]]
        for d in range(1, 1 << b):
            at = first - CUT[d]
            valid = jnp.bitwise_xor(group, d) < group
            outs.append(got[d][at : at + own, :].astype(F32))
            logs.append(jnp.where(valid, got_sums[d][at : at + own, :], NEG))
        best = logs[0]
        for log in logs[1:]:
            best = jnp.maximum(best, log)
        top = jnp.zeros_like(best)
        bottom = jnp.zeros_like(best)
        for out, log in zip(outs, logs):
            weight = jnp.exp2(log - best)
            top = top + weight * out
            bottom = bottom + weight
        compact[first : first + own, :] = top / bottom
        compact_sum[first : first + own, :] = best + jnp.log2(bottom)
    for c in range(ROWS // CHUNK):
        rows = slice(c * CHUNK, (c + 1) * CHUNK)
        outs = [own_out[rows, :]]
        logs = [own_sum[rows, :]]
        for b in range(1, BRANCHES):
            count, dilation = CHUNK >> b, 1 << b
            at = START[b] + c * count
            offset = sm[1 + b]
            place = jnp.where(
                iota((CHUNK, count), 0) == iota((CHUNK, count), 1) * dilation + offset, 1.0, 0.0
            ).astype(BF16)
            out_parts = split3(compact[at : at + count, :])
            log_parts = split3(compact_sum[at : at + count, :])
            first = jnp.concatenate([out_parts[0], log_parts[0]], axis=1)
            second = jnp.concatenate([out_parts[1], log_parts[1]], axis=1)
            spread = jnp.dot(place, first, preferred_element_type=F32)
            spread = spread + jnp.dot(place, second, preferred_element_type=F32)
            log = spread[:, HD:] + jnp.dot(place, log_parts[2], preferred_element_type=F32)
            chosen = lax.rem(iota((CHUNK, HD), 0), dilation) == offset
            outs.append(spread[:, :HD])
            logs.append(jnp.where(chosen, log, NEG))
        best = logs[0]
        for log in logs[1:]:
            best = jnp.maximum(best, log)
        top = jnp.zeros_like(best)
        bottom = jnp.zeros_like(best)
        for out, log in zip(outs, logs):
            weight = jnp.exp2(log - best)
            top = top + weight * out
            bottom = bottom + weight
        merged[rows, :] = (top / bottom).astype(BF16)


def call(kernel, name, sm, operands, outputs, scratch, flops, aliases=None):
    shapes = [jax.ShapeDtypeStruct(shape, dtype) for shape, dtype in outputs]
    moved = sum(math.prod(x.shape) * x.dtype.itemsize for x in list(operands) + shapes)
    return pl.pallas_call(
        kernel,
        name=name,
        out_shape=shapes,
        in_specs=[pl.BlockSpec(memory_space=pltpu.SMEM)]
        + [pl.BlockSpec(memory_space=pltpu.VMEM)] * len(operands),
        out_specs=[pl.BlockSpec(memory_space=pltpu.VMEM)] * len(shapes),
        scratch_shapes=[pltpu.VMEM(shape, dtype) for shape, dtype in scratch],
        input_output_aliases=aliases or {},
        compiler_params=pltpu.CompilerParams(vmem_limit_bytes=32 * 1024 * 1024),
        cost_estimate=pl.CostEstimate(flops=1, bytes_accessed=1, transcendentals=0),
    )(sm, *operands)


def pack(sm, q, k, v):
    return pl.pallas_call(
        pack_kernel,
        name="pack",
        out_shape=[jax.ShapeDtypeStruct((TOTAL, HD), BF16), jax.ShapeDtypeStruct((ROWS, 2 * HD), BF16)],
        in_specs=[pl.BlockSpec(memory_space=pltpu.SMEM)] + [pl.BlockSpec(memory_space=pl.ANY)] * 3,
        out_specs=[pl.BlockSpec(memory_space=pltpu.VMEM)] * 2,
        scratch_shapes=[pltpu.VMEM((ROWS, HD), BF16), pltpu.SemaphoreType.DMA((3,))],
        cost_estimate=pl.CostEstimate(flops=1, bytes_accessed=1, transcendentals=0),
    )(sm, q, k, v)


def place_of(index):
    x, z, core = index // 16, index // 2 % 8, index % 2
    return 2 * x + z // 4, z % 4, core


def index_of(group, z, core):
    return (group // 2 * 8 + group % 2 * 4 + z) * 2 + core


def partner(index, j):
    group, z, core = place_of(index)
    return index_of(group ^ j, z ^ 2 if j % 2 else z, core)


def meet(j):
    return [(index, partner(index, j)) for index in range(64)]


def to_later(j):
    return [(index, other) for index, other in meet(j) if place_of(other)[0] > place_of(index)[0]]


def exchange(step):
    pairs = []
    for index in range(64):
        group, z, core = place_of(index)
        pairs.append((index, index_of(group, z ^ step, core)))
    return pairs


def both_cores(block):
    groups = [[i, i + 1] for i in range(0, 64, 2)]
    return lax.all_gather(block, "seq", axis_index_groups=groups, tiled=True)


def on_device(queries, key_rows, values, offsets):
    seq, head = lax.axis_index("seq"), lax.axis_index("head")
    mine = lax.dynamic_slice_in_dim(offsets, head, 1, axis=1)[:, 0]
    sm = jnp.concatenate([jnp.stack([seq // 8, seq % 8]).astype(jnp.int32), mine[1:], jnp.zeros((3,), jnp.int32)])
    near, kv = pack(sm, queries, key_rows, values)
    keys = [((ROWS, 2 * HD), BF16), ((384, 2 * HD), BF16), ((192, 2 * HD), BF16)]
    state = [((VISITING, 2 * HD), F32), ((ROWS + TOTAL, 2 * HD), F32)]
    work = 4 * HD * 2 * ROWS * 2 * ROWS
    r1 = lax.ppermute(near, "seq", meet(1))
    block2 = lax.ppermute(kv, "seq", exchange(2))
    block1 = lax.ppermute(kv, "seq", exchange(1))
    r2 = lax.ppermute(jnp.concatenate([near[384:], r1[384:]]), "seq", meet(2))
    r4 = lax.ppermute(jnp.concatenate([near[576:], r1[576:], r2[192:288], r2[480:]]), "seq", meet(4))
    pairs = [both_cores(kv), both_cores(block1)]
    block2, r2 = lax.optimization_barrier((block2, r2))
    block3 = lax.ppermute(block2, "seq", exchange(1))
    pairs.append(both_cores(block2))
    early_keys = [((3 * rows, width), dtype) for (rows, width), dtype in keys]
    visiting, cross, own, *early = call(
        early_kernel,
        "three_chips",
        sm,
        pairs + [queries, near, r1, r2, r4],
        [((VISITING, HD), BF16)] + state + early_keys,
        [],
        work,
    )
    block3, own = lax.optimization_barrier((block3, own))
    pairs.append(both_cores(block3))
    crossed = call(
        last_cross_kernel,
        "cross_end",
        sm,
        pairs + [visiting, cross],
        state[:1] + [((message_rows(d)[2], HD), BF16) for d in range(1, GROUPS)] + keys,
        [((VISITING, HD), F32)] + [((message_rows(d)[1] * 128, 128), F32) for d in range(1, GROUPS)],
        work // 2,
        {6: 0},
    )
    back = [lax.ppermute(crossed[j], "seq", to_later(j)) for j in range(1, 6)]
    for j in (6, 7):
        message, back[j - 6] = lax.optimization_barrier((crossed[j], back[j - 6]))
        back.append(lax.ppermute(message, "seq", to_later(j)))
    _, out, log_sum = call(
        last_own_kernel,
        "own_end",
        sm,
        pairs + [queries, near, own] + early + list(crossed[8:]),
        state[1:] + [((ROWS + TOTAL, HD), F32)] * 2,
        keys + [((ROWS + TOTAL, HD), F32)],
        work // 2,
        {7: 0},
    )
    (merged,) = call(
        merge_kernel,
        "merge",
        sm,
        back + [out, log_sum],
        [((ROWS, HD), BF16)],
        [((message_rows(d)[1] * 128, 128), F32) for d in range(1, GROUPS)] + [((TOTAL, HD), F32)] * 2,
        1000000,
    )
    return lax.all_to_all(merged, "head", split_axis=0, concat_axis=1, tiled=True)


def solution(mesh):
    placed = (P("seq", "head"), P("seq", "head"), P("seq", "head"), P())
    return jax.shard_map(
        on_device, mesh=mesh, in_specs=placed, out_specs=P(("seq", "head"), None), check_vma=False
    )
```
